32 devices in a mesh: rep: 4 (over z), fsdp: 8 (over y, x, core).
Axes of the slice: x: 2, y: 2, z: 4, core: 2. Of those that a mesh axis runs over, the one named last changes fastest.
Arguments:
- query_rows: bfloat16 [12288, 3072], P(('rep', 'fsdp')), may hold values from -48 to 48
- key_rows: bfloat16 [12288, 3072], P(('rep', 'fsdp')), may hold values from -48 to 48
- value_rows: bfloat16 [12288, 3072], P(('rep', 'fsdp')), may hold values from -6 to 6
- out_grad: bfloat16 [12288, 3072], P(('rep', 'fsdp')), may hold values from -6 to 6
- out_weight: bfloat16 [3072, 3072], P('fsdp'), may hold values from -0.109375 to 0.109375
- segment_ids: int32 [12288], P(('rep', 'fsdp')), may hold values from -1 to 1023, as said below
Outputs:
- query_grad: bfloat16 [12288, 3072], P(('rep', 'fsdp'))
- key_grad: bfloat16 [12288, 3072], P(('rep', 'fsdp'))
- value_grad: bfloat16 [12288, 3072], P(('rep', 'fsdp'))
- weight_grad: float32 [3072, 3072], P('fsdp')
The draws below stay inside these ranges and needn't reach their ends.
Inputs may be any that keep to these rules, and one draw needn't show every extreme that they name: `segment_ids`: each aligned block of 384 rows holds whole images in contiguous runs of rows followed by padding rows with id -1; an image id appears in no other block; every image and every block's live part has a multiple of 12 rows, at least 4 such units live a block; in each aligned run of 8 blocks exactly one block has no padding, and every other block has at most 192 live rows.
All inputs are finite; a program needn't handle non-finite values.
Results may differ from the reference program's by a relative error of at most 0.02.
Values may be sent and summed in bfloat16 or wider, within the bound.
No kernel may reach another device: no remote copies, remote signals or barrier semaphores. Data moves between devices by JAX's collectives and lax.ppermute only.
A program may use at most 192 MiB of HBM per device.

```python
import math
import jax
import jax.numpy as jnp
from jax import lax

H = 24
E = 128
DW = 3072
ROWS_DEV = 384
HD = 3072
ROWS_ALL = 12288
N_FSDP = 8


def drawn_pair(key):
    base = jax.random.fold_in(key, 7)
    keys_split = jax.random.split(base, 2)
    width = H * E
    shape = (ROWS_ALL, width)
    query_out = jnp.clip(jax.random.normal(keys_split[0], shape, jnp.float32), -4.0, 4.0)
    key_out = jnp.clip(jax.random.normal(keys_split[1], shape, jnp.float32), -4.0, 4.0)
    return (query_out, key_out)


def draw_query_rows(key, part):
    return drawn_pair(key)[0].astype(jnp.bfloat16)


def draw_key_rows(key, part):
    return drawn_pair(key)[1].astype(jnp.bfloat16)


def draw_segment_ids(key, part):
    base = jax.random.fold_in(key, 11)
    keys_split = jax.random.split(base, 3)
    block_count = ROWS_ALL // ROWS_DEV
    unit_rows = ROWS_DEV // 32
    live_rows = unit_rows * jax.random.randint(keys_split[0], (block_count,), 4, 17)
    full_member = jax.random.randint(keys_split[1], (block_count // N_FSDP,), 0, N_FSDP)
    is_full = jnp.arange(block_count) % N_FSDP == jnp.repeat(full_member, N_FSDP)
    live_rows = jnp.where(is_full, ROWS_DEV, live_rows)
    lengths = unit_rows * jax.random.randint(keys_split[2], (block_count, 32), 1, 17)
    bounds = jnp.cumsum(lengths, axis=1)
    positions = jnp.arange(ROWS_DEV)
    local_ids = jnp.sum((bounds[:, None, :] <= positions[None, :, None]).astype(jnp.int32), axis=2)
    ids = jnp.arange(block_count)[:, None] * 32 + (31 - local_ids)
    ids = jnp.where(positions[None, :] < live_rows[:, None], ids, -1)
    return ids.reshape(ROWS_ALL).astype(jnp.int32)


def level_of(key, shape, cuts, smallest, top_value):
    gain, own = 1.0, jax.random.fold_in(key, 6)
    for position, parts in cuts:
        heights = jnp.exp(jax.random.uniform(jax.random.fold_in(own, position), (parts,), jnp.float32, smallest / len(cuts), top_value / len(cuts)))
        gain = gain * jnp.repeat(heights, shape[position] // parts).reshape([-1 if axis == position else 1 for axis in range(len(shape))])
    return gain


def noise(own_key, extent, deviation, limit, cuts=(), held_as=jnp.bfloat16):
    factor_of = level_of(own_key, extent, cuts, -0.22, 0.18) if cuts else 1.0
    result = jax.random.normal(own_key, extent, jnp.float32) * deviation * factor_of
    return jnp.minimum(jnp.maximum(result, -limit), limit).astype(held_as)


def setup_inputs(seed: int = 0) -> dict:
    arg_keys = jax.random.split(jax.random.key(seed), 7)
    return {
        "query_rows": draw_query_rows(jax.random.fold_in(arg_keys[6], 71), 0),
        "key_rows": draw_key_rows(jax.random.fold_in(arg_keys[6], 71), 0),
        "value_rows": noise(arg_keys[2], (ROWS_ALL, HD), 1.0, 6.0, ((0, 32),)),
        "out_grad": noise(arg_keys[3], (ROWS_ALL, DW), 1.0, 6.0, ((0, 32),)),
        "out_weight": noise(arg_keys[4], (HD, DW), (H * E) ** -0.5, 0.109375, ((0, 8),)),
        "segment_ids": draw_segment_ids(jax.random.fold_in(arg_keys[6], 71), 0),
    }


def attention_grads(query_block, key_block, value_block, grad_block, query_segments, key_segments):
    query_count = query_block.shape[0]
    key_count = key_block.shape[0]
    head_count = query_block.shape[1] // E
    inverse_root = 1.0 / math.sqrt(E)
    query_heads = query_block.reshape(query_count, head_count, E).astype(jnp.float32)
    key_heads = key_block.reshape(key_count, head_count, E).astype(jnp.float32)
    value_heads = value_block.reshape(key_count, head_count, E).astype(jnp.float32)
    grad_heads = grad_block.reshape(query_count, head_count, E).astype(jnp.float32)
    logits = jnp.einsum('qhe,khe->hqk', query_heads, key_heads) * inverse_root
    allowed = (query_segments[:, None] == key_segments[None, :]) & (query_segments[:, None] >= 0)
    masked = jnp.where(allowed[None], logits, -1e+30)
    row_max = lax.optimization_barrier(jnp.max(masked, axis=2, keepdims=True))
    raw_weights = jnp.where(allowed[None], jnp.exp(masked - row_max), 0.0)
    totals = lax.optimization_barrier(jnp.sum(raw_weights, axis=2, keepdims=True))
    totals = jnp.where((query_segments >= 0)[None, :, None], totals, 1.0)
    probs = raw_weights / totals
    probs_half = probs.astype(jnp.bfloat16).astype(jnp.float32)
    attended = jnp.einsum('hqk,khe->qhe', probs_half, value_heads).astype(jnp.bfloat16)
    attended_wide = attended.astype(jnp.float32)
    grad_probs = jnp.einsum('qhe,khe->hqk', grad_heads, value_heads)
    row_dot = jnp.einsum('qhe,qhe->hq', grad_heads, attended_wide)
    grad_logits = (probs * (grad_probs - row_dot[:, :, None])).astype(jnp.bfloat16).astype(jnp.float32)
    grad_query = jnp.einsum('hqk,khe->qhe', grad_logits, key_heads) * inverse_root
    grad_key = jnp.einsum('hqk,qhe->khe', grad_logits, query_heads) * inverse_root
    grad_value = jnp.einsum('hqk,qhe->khe', probs_half, grad_heads)
    return (attended.reshape(query_count, -1), grad_query.reshape(query_count, -1), grad_key.reshape(key_count, -1), grad_value.reshape(key_count, -1))

def reference(query_rows, key_rows, value_rows, out_grad, out_weight, segment_ids):
    block_count = ROWS_ALL // ROWS_DEV
    feature_count = query_rows.shape[1]

    def one_block(totals, inputs):
        query_block, key_block, value_block, grad_block, segment_block = inputs
        grad_attended = jnp.dot(grad_block, out_weight.T, preferred_element_type=jnp.float32).astype(jnp.bfloat16)
        attended, grad_query, grad_key, grad_value = attention_grads(query_block, key_block, value_block, grad_attended, segment_block, segment_block)
        term_half = jnp.dot(attended.T, grad_block, preferred_element_type=jnp.float32).astype(jnp.bfloat16)
        term_half = lax.optimization_barrier(term_half)
        totals = totals + term_half.astype(jnp.float32)
        return (totals, (grad_query.astype(jnp.bfloat16), grad_key.astype(jnp.bfloat16), grad_value.astype(jnp.bfloat16)))
    inputs = (query_rows.reshape(block_count, ROWS_DEV, feature_count), key_rows.reshape(block_count, ROWS_DEV, feature_count), value_rows.reshape(block_count, ROWS_DEV, feature_count), out_grad.reshape(block_count, ROWS_DEV, out_grad.shape[1]), segment_ids.reshape(block_count, ROWS_DEV))
    start_totals = jnp.zeros((feature_count, out_grad.shape[1]), jnp.float32)
    totals, grads = lax.scan(one_block, start_totals, inputs)
    query_grad = grads[0].reshape(ROWS_ALL, feature_count)
    key_grad = grads[1].reshape(ROWS_ALL, feature_count)
    value_grad = grads[2].reshape(ROWS_ALL, feature_count)
    weight_grad = totals * (1.0 / math.sqrt(ROWS_ALL))
    return (query_grad, key_grad, value_grad, weight_grad)
```

```python
import functools
import math

import jax
import jax.numpy as jnp
from jax import lax
from jax.experimental import pallas as pl
from jax.experimental.pallas import tpu as pltpu
from jax.sharding import PartitionSpec as P

E = 128
BLOCK_HEADS = 3
BLOCK = BLOCK_HEADS * E
PARTS = 2
SUM_PARTS = 4
F32 = jnp.float32
BF16 = jnp.bfloat16
LOG2_E = math.log2(math.e)
FAR = -1e30
VMEM_LIMIT = 48 * 1024 * 1024


def dot(a, b, a_dim, b_dim):
    return lax.dot_general(a, b, (((a_dim,), (b_dim,)), ((), ())), preferred_element_type=F32)


def forward_kernel(order, ids_column, ids_row, query, key, value, attended, weights, bias):
    @pl.when(pl.program_id(0) == 0)
    def _():
        allowed = (ids_column[...] == ids_row[...]) & (ids_column[...] >= 0)
        bias[...] = jnp.where(allowed, 0.0, FAR)

    scale = LOG2_E / math.sqrt(E)
    for head in range(BLOCK_HEADS):
        columns = slice(head * E, (head + 1) * E)
        logits = dot(key[:, columns], query[:, columns], 1, 1) * scale + bias[...]
        top = jnp.maximum(jnp.max(logits, axis=0, keepdims=True), 0.5 * FAR)
        raw = jnp.exp2(logits - top)
        total = jnp.sum(raw, axis=0, keepdims=True)
        half = (raw * (1.0 / jnp.maximum(total, 0.5))).astype(BF16)
        weights[head] = half
        attended[:, columns] = dot(half, value[:, columns], 0, 0).astype(BF16)


def forward(order, segment_ids, query_rows, key_rows, value_rows):
    rows, width = query_rows.shape
    blocks = width // BLOCK
    absolute = pl.BlockSpec((rows, BLOCK), lambda j, order: (0, order[j]))
    return pl.pallas_call(
        forward_kernel,
        grid_spec=pltpu.PrefetchScalarGridSpec(
            num_scalar_prefetch=1,
            grid=(blocks,),
            in_specs=[
                pl.BlockSpec((rows, 1), lambda j, order: (0, 0)),
                pl.BlockSpec((1, rows), lambda j, order: (0, 0)),
                absolute,
                absolute,
                absolute,
            ],
            out_specs=[
                pl.BlockSpec((rows, BLOCK), lambda j, order: (0, j)),
                pl.BlockSpec((BLOCK_HEADS, rows, rows), lambda j, order: (j, 0, 0)),
            ],
            scratch_shapes=[pltpu.VMEM((rows, rows), F32)],
        ),
        out_shape=[
            jax.ShapeDtypeStruct((rows, width), BF16),
            jax.ShapeDtypeStruct((width // E, rows, rows), BF16),
        ],
        compiler_params=pltpu.CompilerParams(vmem_limit_bytes=VMEM_LIMIT),
        cost_estimate=pl.CostEstimate(
            flops=4 * rows * rows * width,
            bytes_accessed=8 * rows * width + 2 * rows * rows * (width // E),
            transcendentals=rows * rows * (width // E),
        ),
        name="attention_forward",
    )(order, segment_ids.reshape(rows, 1), segment_ids.reshape(1, rows), query_rows, key_rows, value_rows)


def backward_kernel(
    order, grad_main, grad_low, grad_high, query, key, value, weights, grad_query, grad_key, grad_value
):
    grad_all = jnp.concatenate([grad_main[...], grad_low[...], grad_high[...]], axis=0)
    inverse_root = 1.0 / math.sqrt(E)
    for head in range(BLOCK_HEADS):
        columns = slice(head * E, (head + 1) * E)
        grad = grad_all[:, columns]
        half = weights[head]
        grad_probs = dot(value[:, columns], grad, 1, 1)
        wide = half.astype(F32)
        row_dot = jnp.sum(wide * grad_probs, axis=0, keepdims=True)
        grad_logits = (wide * (grad_probs - row_dot)).astype(BF16)
        grad_value[:, columns] = dot(half, grad, 1, 0).astype(BF16)
        grad_key[:, columns] = (dot(grad_logits, query[:, columns], 1, 0) * inverse_root).astype(BF16)
        grad_query[:, columns] = (dot(grad_logits, key[:, columns], 0, 0) * inverse_root).astype(BF16)


def backward(order, grad_main, grad_low, grad_high, query_rows, key_rows, value_rows, weights):
    rows, width = query_rows.shape
    blocks = width // BLOCK
    absolute = pl.BlockSpec((rows, BLOCK), lambda j, order: (0, order[j]))

    def relative(a):
        return pl.BlockSpec((a.shape[0], BLOCK), lambda j, order: (0, j))

    return pl.pallas_call(
        backward_kernel,
        grid_spec=pltpu.PrefetchScalarGridSpec(
            num_scalar_prefetch=1,
            grid=(blocks,),
            in_specs=[
                relative(grad_main),
                relative(grad_low),
                relative(grad_high),
                absolute,
                absolute,
                absolute,
                pl.BlockSpec((BLOCK_HEADS, rows, rows), lambda j, order: (j, 0, 0)),
            ],
            out_specs=[absolute, absolute, absolute],
        ),
        out_shape=[jax.ShapeDtypeStruct((rows, width), BF16)] * 3,
        compiler_params=pltpu.CompilerParams(vmem_limit_bytes=VMEM_LIMIT),
        cost_estimate=pl.CostEstimate(
            flops=8 * rows * rows * width,
            bytes_accessed=14 * rows * width + 2 * rows * rows * (width // E),
            transcendentals=0,
        ),
        name="attention_backward",
    )(order, grad_main, grad_low, grad_high, query_rows, key_rows, value_rows, weights)


def sum_over_line(part):
    place = lax.axis_index("rep")
    in_middle = (place == 1) | (place == 2)
    arrived = lax.ppermute(part, "rep", [(0, 1), (3, 2)])
    pair = (part.astype(F32) + arrived.astype(F32)).astype(BF16)
    arrived = lax.ppermute(pair, "rep", [(1, 2), (2, 1)])
    total = (pair.astype(F32) + arrived.astype(F32)).astype(BF16)
    arrived = lax.ppermute(total, "rep", [(1, 0), (2, 3)])
    return jnp.where(in_middle, total, arrived).astype(F32)


def pairwise(query_rows, key_rows, value_rows, out_grad, out_weight, segment_ids):
    rows, width = query_rows.shape
    short = rows // 2
    quarter = short // 2
    me = lax.axis_index("fsdp")
    core = me % 2
    order = me ^ jnp.arange(8, dtype=jnp.int32)

    def swap(a, mask):
        return lax.ppermute(a, "fsdp", [(f, f ^ mask) for f in range(8)])

    def own_half(a):
        low, high = a[:quarter], a[quarter:]
        return jnp.where(core == 0, low, high), jnp.where(core == 0, high, low)

    live_ids = segment_ids[short:] >= 0
    main = out_grad[:short]
    extra = jnp.where(live_ids[:, None], out_grad[short:], jnp.zeros((), BF16))

    attended, weights = forward(order, segment_ids, query_rows, key_rows, value_rows)

    part_width = width // PARTS
    planes, others = [], []
    for part in range(PARTS):
        columns = slice(part * part_width, (part + 1) * part_width)
        here, there = own_half(extra[:, columns])
        here = here + swap(there, 1)
        cut = quarter // 2
        mine = main[:, columns]
        from_x = swap(jnp.concatenate([mine, here[:cut]]), 2)
        from_y = swap(jnp.concatenate([mine, here[cut:]]), 4)
        first = here[:cut] + from_x[short:]
        second = here[cut:] + from_y[short:]
        via_y = swap(jnp.concatenate([from_x[:quarter], first]), 4)
        via_x = swap(jnp.concatenate([from_y[quarter:short], second]), 2)
        plane = jnp.concatenate(
            [
                mine,
                from_x[:short],
                from_y[:short],
                via_y[:quarter],
                via_x[:quarter],
                first + via_y[quarter:],
                second + via_x[quarter:],
            ]
        )
        planes.append(plane)
        others.append(swap(plane, 1))

    here, there = own_half(attended[short:])
    there = jnp.concatenate([there[:, (j ^ 1) * BLOCK : ((j ^ 1) + 1) * BLOCK] for j in range(8)], axis=1)
    here = here + swap(there, 1)
    both = jnp.concatenate([attended[:short], here])
    pair_width = 2 * BLOCK
    kept = both[:, :pair_width]
    arrived = [swap(both[:, m // 2 * pair_width : (m // 2 + 1) * pair_width], m) for m in (2, 4, 6)]
    pieces = [a[:short] for a in [kept] + arrived]
    pieces.append(kept[short:] + arrived[0][short:] + arrived[1][short:] + arrived[2][short:])
    gathered = jnp.concatenate(pieces)
    attended_plane = gathered[:, :BLOCK]
    attended_other = swap(gathered[:, BLOCK:], 1)

    root = 1.0 / math.sqrt(rows * lax.axis_size("fsdp") * lax.axis_size("rep"))
    sums = []
    for part in range(PARTS):
        term = dot(attended_plane, planes[part], 0, 0) + dot(attended_other, others[part], 0, 0)
        term = term.astype(BF16)
        sub = SUM_PARTS // PARTS
        sub_width = part_width // sub
        for i in range(sub):
            sums.append(sum_over_line(term[:, i * sub_width : (i + 1) * sub_width]) * root)
    weight_grad = jnp.concatenate(sums, axis=1)

    grad_plane, grad_other = 0.0, 0.0
    for part in range(PARTS):
        weight_part = out_weight[:, part * part_width : (part + 1) * part_width]
        grad_other = grad_other + dot(others[part], weight_part, 1, 1)
        grad_plane = grad_plane + dot(planes[part], weight_part, 1, 1)
    grad = jnp.concatenate([grad_plane.astype(BF16), swap(grad_other.astype(BF16), 1)], axis=1)
    tail = grad[4 * short :]
    moved = [
        swap(jnp.concatenate([grad[i * short : (i + 1) * short], tail]), 2 * i) for i in (1, 2, 3)
    ]
    whole = jnp.concatenate([jnp.concatenate([grad[:short], tail])] + moved, axis=1)
    tail = whole[short:]
    tail_other = swap(tail, 1)
    tail_other = jnp.concatenate(
        [tail_other[:, (j ^ 1) * BLOCK : ((j ^ 1) + 1) * BLOCK] for j in range(8)], axis=1
    )
    low = jnp.where(core == 0, tail, tail_other)
    high = jnp.where(core == 0, tail_other, tail)
    grads = backward(order, whole[:short], low, high, query_rows, key_rows, value_rows, weights)
    return (*grads, weight_grad)


def general(query_rows, key_rows, value_rows, out_grad, out_weight, segment_ids):
    rows, width = query_rows.shape
    short = rows // 2
    count = lax.axis_size("fsdp")
    order = jnp.arange(width // BLOCK, dtype=jnp.int32)
    extra = jnp.where((segment_ids[short:] >= 0)[:, None], out_grad[short:], jnp.zeros((), BF16))
    attended, weights = forward(order, segment_ids, query_rows, key_rows, value_rows)
    live = jnp.concatenate(
        [lax.all_gather(out_grad[:short], "fsdp", axis=0, tiled=True), lax.psum(extra, "fsdp")]
    )
    attended_live = jnp.concatenate(
        [
            lax.all_to_all(attended[:short], "fsdp", split_axis=1, concat_axis=0, tiled=True),
            lax.psum_scatter(attended[short:], "fsdp", scatter_dimension=1, tiled=True),
        ]
    )
    term = dot(attended_live, live, 0, 0).astype(BF16)
    total = lax.psum(term, "rep").astype(F32)
    grad = dot(live, out_weight, 1, 1).astype(BF16)
    grad_main = lax.all_to_all(
        grad[: count * short], "fsdp", split_axis=0, concat_axis=1, tiled=True
    )
    grad_extra = lax.all_gather(grad[count * short :], "fsdp", axis=1, tiled=True)
    half = short // 2
    grads = backward(
        order, grad_main, grad_extra[:half], grad_extra[half:], query_rows, key_rows, value_rows, weights
    )
    return (*grads, total * (1.0 / math.sqrt(rows * count * lax.axis_size("rep"))))


def solution(mesh):
    fits = mesh.shape["fsdp"] == 8 and mesh.shape["rep"] == 4
    split = P(("rep", "fsdp"), None)
    return jax.shard_map(
        pairwise if fits else general,
        mesh=mesh,
        in_specs=(split, split, split, split, P("fsdp", None), P(("rep", "fsdp"))),
        out_specs=(split, split, split, P("fsdp", None)),
        check_vma=False,
    )
```

```python
import functools
import math

import jax
import jax.numpy as jnp
from jax import lax
from jax.experimental import pallas as pl
from jax.experimental.pallas import tpu as pltpu
from jax.sharding import PartitionSpec as P

E = 128
BLOCK_HEADS = 3
BLOCK = BLOCK_HEADS * E
PAIR = 2 * BLOCK
PARTS = 3
F32 = jnp.float32
BF16 = jnp.bfloat16
LOG2_E = math.log2(math.e)
FAR = -1e30
VMEM_LIMIT = 24 * 1024 * 1024
ATTENTION_VMEM_LIMIT = 40 * 1024 * 1024
NO_COST = pl.CostEstimate(flops=0, bytes_accessed=0, transcendentals=0)


def dot(a, b, a_dim, b_dim):
    return lax.dot_general(a, b, (((a_dim,), (b_dim,)), ((), ())), preferred_element_type=F32)


def forward_kernel(order, ids_column, ids_row, query, key, value, attended, there, weights, bias):
    @pl.when(pl.program_id(0) == 0)
    def _():
        allowed = (ids_column[...] == ids_row[...]) & (ids_column[...] >= 0)
        bias[...] = jnp.where(allowed, 0.0, FAR)

    scale = LOG2_E / math.sqrt(E)
    columns = [slice(head * E, (head + 1) * E) for head in range(BLOCK_HEADS)]
    logits = [dot(key[:, c], query[:, c], 1, 1) * scale + bias[...] for c in columns]
    halves = []
    for head in range(BLOCK_HEADS):
        top = jnp.maximum(jnp.max(logits[head], axis=0, keepdims=True), 0.5 * FAR)
        raw = jnp.exp2(logits[head] - top)
        total = jnp.sum(raw, axis=0, keepdims=True)
        half = (raw * (1.0 / jnp.maximum(total, 0.5))).astype(BF16)
        weights[head] = half
        halves.append(half)
    for head in range(BLOCK_HEADS):
        attended[:, columns[head]] = dot(halves[head], value[:, columns[head]], 0, 0).astype(BF16)
    quarter = there.shape[0]
    start = pl.multiple_of((3 - order[0] % 2) * quarter, 32)
    there[...] = attended[pl.ds(start, quarter), :]


def forward(order, segment_ids, query_rows, key_rows, value_rows):
    rows = query_rows.shape[0]
    blocks = order.shape[0]
    heads = blocks * BLOCK_HEADS
    absolute = pl.BlockSpec((rows, BLOCK), lambda j, order: (0, order[j]))
    return pl.pallas_call(
        forward_kernel,
        grid_spec=pltpu.PrefetchScalarGridSpec(
            num_scalar_prefetch=1,
            grid=(blocks,),
            in_specs=[
                pl.BlockSpec((rows, 1), lambda j, order: (0, 0)),
                pl.BlockSpec((1, rows), lambda j, order: (0, 0)),
                absolute,
                absolute,
                absolute,
            ],
            out_specs=[
                pl.BlockSpec((rows, BLOCK), lambda j, order: (0, j)),
                pl.BlockSpec((rows // 4, BLOCK), lambda j, order: (0, j ^ 1)),
                pl.BlockSpec((BLOCK_HEADS, rows, rows), lambda j, order: (j, 0, 0)),
            ],
            scratch_shapes=[pltpu.VMEM((rows, rows), F32)],
        ),
        out_shape=[
            jax.ShapeDtypeStruct((rows, blocks * BLOCK), BF16),
            jax.ShapeDtypeStruct((rows // 4, blocks * BLOCK), BF16),
            jax.ShapeDtypeStruct((heads, rows, rows), BF16),
        ],
        compiler_params=pltpu.CompilerParams(vmem_limit_bytes=ATTENTION_VMEM_LIMIT),
        cost_estimate=NO_COST,
        name="attention_forward",
    )(order, segment_ids.reshape(rows, 1), segment_ids.reshape(1, rows), query_rows, key_rows, value_rows)


def backward_kernel(order, grad_main, grad_here, grad_there, query, key, value, weights, *rest):
    grad_query, grad_key, grad_value = rest[-3:]
    first = order[0] % 2 == 0
    here, there = grad_here[...], grad_there[...]
    grad_all = jnp.concatenate(
        [grad_main[...], jnp.where(first, here, there), jnp.where(first, there, here)], axis=0
    )
    inverse_root = 1.0 / math.sqrt(E)
    for head in range(BLOCK_HEADS):
        columns = slice(head * E, (head + 1) * E)
        grad = grad_all[:, columns]
        half = weights[head]
        grad_probs = dot(value[:, columns], grad, 1, 1)
        wide = half.astype(F32)
        row_dot = jnp.sum(wide * grad_probs, axis=0, keepdims=True)
        grad_logits = (wide * (grad_probs - row_dot)).astype(BF16)
        grad_value[:, columns] = dot(half, grad, 1, 0).astype(BF16)
        grad_key[:, columns] = (dot(grad_logits, query[:, columns], 1, 0) * inverse_root).astype(BF16)
        grad_query[:, columns] = (dot(grad_logits, key[:, columns], 0, 0) * inverse_root).astype(BF16)


def backward(order, grad, there, flip, there_skip, query_rows, key_rows, value_rows, weights, skip, done):
    rows, width = query_rows.shape
    quarter = there.shape[0]
    blocks = order.shape[0]
    heads = blocks * BLOCK_HEADS
    absolute = pl.BlockSpec((rows, BLOCK), lambda j, order: (0, order[j]))
    shapes = [jax.ShapeDtypeStruct((rows, width), BF16)] * 3
    return pl.pallas_call(
        backward_kernel,
        grid_spec=pltpu.PrefetchScalarGridSpec(
            num_scalar_prefetch=1,
            grid=(blocks,),
            in_specs=[
                pl.BlockSpec((2 * quarter, BLOCK), lambda j, order: (0, j)),
                pl.BlockSpec((quarter, BLOCK), lambda j, order: (2, j)),
                pl.BlockSpec((quarter, BLOCK), lambda j, order: (0, (j ^ flip) + there_skip)),
                absolute,
                absolute,
                absolute,
                pl.BlockSpec((BLOCK_HEADS, rows, rows), lambda j, order: (j + skip, 0, 0)),
            ]
            + [pl.BlockSpec(memory_space=pl.ANY)] * len(done),
            out_specs=[absolute, absolute, absolute],
        ),
        out_shape=shapes,
        input_output_aliases={8 + i: i for i in range(len(done))},
        compiler_params=pltpu.CompilerParams(vmem_limit_bytes=ATTENTION_VMEM_LIMIT),
        cost_estimate=NO_COST,
        name="attention_backward",
    )(order, grad, grad, there, query_rows, key_rows, value_rows, weights, *done)


def whole(kernel, shapes, *arrays, scalars=(), name):
    vmem, smem = pl.BlockSpec(memory_space=pltpu.VMEM), pl.BlockSpec(memory_space=pltpu.SMEM)
    return pl.pallas_call(
        kernel,
        in_specs=[smem] * len(scalars) + [vmem] * len(arrays),
        out_specs=[vmem] * len(shapes),
        out_shape=[jax.ShapeDtypeStruct(shape, BF16) for shape in shapes],
        compiler_params=pltpu.CompilerParams(vmem_limit_bytes=VMEM_LIMIT),
        cost_estimate=NO_COST,
        name=name,
    )(*scalars, *arrays)


def other_quarter_kernel(blocks, ids, extra, out):
    is_full = ids[ids.shape[0] - 1] >= 0
    out[...] = jnp.where(is_full, extra[...], jnp.zeros((), BF16))


def other_quarter(blocks, ids, rows):
    count, width = rows.shape
    quarter = count // 4
    return pl.pallas_call(
        other_quarter_kernel,
        grid_spec=pltpu.PrefetchScalarGridSpec(
            num_scalar_prefetch=2,
            grid=(1,),
            in_specs=[pl.BlockSpec((quarter, width), lambda i, blocks, ids: (3 - blocks[0] % 2, 0))],
            out_specs=pl.BlockSpec((quarter, width), lambda i, blocks, ids: (0, 0)),
        ),
        out_shape=jax.ShapeDtypeStruct((quarter, width), BF16),
        compiler_params=pltpu.CompilerParams(vmem_limit_bytes=ATTENTION_VMEM_LIMIT),
        cost_estimate=NO_COST,
        name="other_quarter",
    )(blocks, ids, rows)


def gather_start_kernel(blocks, ids, rows, arrived, *outs):
    quarter = arrived.shape[0]
    short, cut = 2 * quarter, quarter // 2
    is_full = ids[ids.shape[0] - 1] >= 0
    start = pl.multiple_of(short + quarter * (blocks[0] % 2), 32)
    own = jnp.where(is_full, rows[pl.ds(start, quarter), :], jnp.zeros((), BF16))
    here = own + arrived[...]
    width = outs[0].shape[1]
    for part in range(len(outs) // 2):
        columns = slice(part * width, (part + 1) * width)
        for i in range(2):
            outs[2 * part + i][:short] = rows[:short, columns]
            outs[2 * part + i][short:] = here[i * cut : (i + 1) * cut, columns]


def gather_forward_kernel(to_x, to_y, from_x, from_y, next_y, next_x):
    quarter = from_x.shape[0] * 2 // 5
    short = 2 * quarter
    next_y[:quarter] = from_x[:quarter]
    next_x[:quarter] = from_y[quarter:short]
    next_y[quarter:] = to_x[short:] + from_x[short:]
    next_x[quarter:] = to_y[short:] + from_y[short:]


def gather_end_kernel(to_x, from_x, from_y, next_y, next_x, via_y, via_x, plane):
    quarter = to_x.shape[0] * 2 // 5
    short, cut = 2 * quarter, quarter // 2
    plane[:short] = to_x[:short]
    plane[short : 2 * short] = from_x[:short]
    plane[2 * short : 3 * short] = from_y[:short]
    plane[3 * short : 3 * short + quarter] = via_y[:quarter]
    plane[3 * short + quarter : 4 * short] = via_x[:quarter]
    plane[4 * short : 4 * short + cut] = next_y[quarter:] + via_y[quarter:]
    plane[4 * short + cut :] = next_x[quarter:] + via_x[quarter:]


def pack_kernel(blocks, attended, arrived, *outs):
    quarter = arrived.shape[0]
    short = 2 * quarter
    start = pl.multiple_of(short + quarter * (blocks[0] % 2), 32)
    extra = attended[pl.ds(start, quarter), :] + arrived[...]
    for i, out in enumerate(outs):
        columns = slice(i * PAIR, (i + 1) * PAIR)
        out[:short] = attended[:short, columns]
        out[short:] = extra[:, columns]


def collect_kernel(kept, from_x, from_y, from_far, gathered):
    short = kept.shape[0] * 2 // 3
    parts = [kept, from_x, from_y, from_far]
    for i, part in enumerate(parts):
        gathered[i * short : (i + 1) * short] = part[:short]
    gathered[4 * short :] = (kept[short:] + from_x[short:]) + (from_y[short:] + from_far[short:])


def term_other_kernel(attended, plane, *outs):
    share = dot(attended[:, BLOCK:], plane[...], 0, 0).astype(BF16)
    width = share.shape[1] // len(outs)
    for i, out in enumerate(outs):
        out[...] = share[:, i * width : (i + 1) * width]


def term_own_kernel(attended, plane, left, right, *outs):
    own = dot(attended[:, :BLOCK], plane[...], 0, 0)
    width = left.shape[1]
    total = [(own[:, :width] + left[...].astype(F32)).astype(BF16), (own[:, width:] + right[...].astype(F32)).astype(BF16)]
    for i in range(2):
        if len(outs) == 2:
            outs[i][...] = total[i]
        else:
            outs[0][:, i * width : (i + 1) * width] = total[i]


def grad_kernel(plane, own, other, *rest):
    for i, weight in enumerate((own, other)):
        columns = slice(i * BLOCK, (i + 1) * BLOCK)
        share = dot(plane[...], weight[...], 1, 1)
        if len(rest) == 2:
            share = rest[0][:, columns] + share
        rest[-1][:, columns] = share


def grad_end_kernel(plane, own, other, before, *pieces):
    rows = pieces[0].shape[0]
    short = rows * 2 // 3
    for i, weight in enumerate((own, other)):
        columns = slice(i * BLOCK, (i + 1) * BLOCK)
        total = (before[:, columns] + dot(plane[...], weight[...], 1, 1)).astype(BF16)
        for j, piece in enumerate(pieces):
            piece[:short, columns] = total[j * short : (j + 1) * short]
            piece[short:, columns] = total[4 * short :]


def grad_part(part, plane, own_weight, other_weight, before):
    count, width = plane.shape
    weight = pl.BlockSpec((BLOCK, width), lambda i: (0, part))
    result = pl.BlockSpec((count, PAIR), lambda i: (0, 0))
    last = part == PARTS - 1
    rows = count // 3
    piece = pl.BlockSpec((rows, PAIR), lambda i: (0, 0))
    return pl.pallas_call(
        grad_end_kernel if last else grad_kernel,
        grid=(1,),
        in_specs=[pl.BlockSpec((count, width), lambda i: (0, 0)), weight, weight] + [result] * len(before),
        out_specs=[piece] * 4 if last else [result],
        out_shape=[jax.ShapeDtypeStruct((rows, PAIR), BF16)] * 4
        if last
        else [jax.ShapeDtypeStruct((count, PAIR), F32)],
        compiler_params=pltpu.CompilerParams(vmem_limit_bytes=VMEM_LIMIT),
        cost_estimate=NO_COST,
        name="grad_attended",
    )(plane, own_weight, other_weight, *before)


def add_kernel(a, b, out):
    out[...] = (a[...].astype(F32) + b[...].astype(F32)).astype(BF16)


class Order:
    def __init__(self):
        self.last = ()

    def __call__(self, *arrays):
        held = lax.optimization_barrier((*self.last, *arrays))[len(self.last) :]
        return held[0] if len(held) == 1 else held

    def mark(self, *arrays):
        self.last = tuple(arrays)


def add(a, b):
    return whole(add_kernel, [a.shape], a, b, name="add")[0]


def line_end_kernel(scale, place, total, arrived, *rest):
    in_middle = (place[0] == 1) | (place[0] == 2)
    rest[-1][...] = jnp.where(in_middle, total[...], arrived[...]).astype(F32) * scale


def line_end(scale, place, total, arrived, start, all_width, done):
    rows, width = total.shape
    piece = pl.BlockSpec((rows, width), lambda i, place: (0, 0))
    return pl.pallas_call(
        functools.partial(line_end_kernel, scale),
        grid_spec=pltpu.PrefetchScalarGridSpec(
            num_scalar_prefetch=1,
            grid=(1,),
            in_specs=[piece, piece] + [pl.BlockSpec(memory_space=pl.ANY)] * len(done),
            out_specs=pl.BlockSpec((rows, width), lambda i, place: (0, start // width)),
        ),
        out_shape=jax.ShapeDtypeStruct((rows, all_width), F32),
        input_output_aliases={3 + i: i for i in range(len(done))},
        compiler_params=pltpu.CompilerParams(vmem_limit_bytes=VMEM_LIMIT),
        cost_estimate=NO_COST,
        name="line_end",
    )(place, total, arrived, *done)


class LineSum:
    def __init__(self, order, scale, width):
        self.order, self.scale, self.width = order, scale, width
        self.place = lax.axis_index("rep").astype(jnp.int32).reshape(1)
        self.held, self.arriving, self.done = {}, {}, ()

    def start(self, piece, part):
        self.held[piece] = part
        self.arriving[piece] = lax.ppermute(part, "rep", [(0, 1), (3, 2)])

    def across(self, piece):
        part, arrived = self.order(self.held[piece], self.arriving[piece])
        pair = add(part, arrived)
        self.order.mark(pair)
        self.held[piece] = pair
        self.arriving[piece] = lax.ppermute(pair, "rep", [(1, 2), (2, 1)])

    def back(self, piece):
        pair, arrived = self.order(self.held[piece], self.arriving[piece])
        total = add(pair, arrived)
        self.order.mark(total)
        self.held[piece] = total
        self.arriving[piece] = lax.ppermute(total, "rep", [(1, 0), (2, 3)])

    def finish(self, piece, start):
        held = self.order(self.held[piece], self.arriving[piece], *self.done)
        result = line_end(self.scale, self.place, held[0], held[1], start, self.width, held[2:])
        self.order.mark(result)
        self.done = (result,)


def pairwise(query_rows, key_rows, value_rows, out_grad, out_weight, segment_ids):
    rows, width = query_rows.shape
    short = rows // 2
    quarter = short // 2
    cut = quarter // 2
    part_width = width // PARTS
    me = lax.axis_index("fsdp")
    core = me % 2
    blocks = me ^ jnp.arange(8, dtype=jnp.int32)
    order = Order()
    line = LineSum(order, 1.0 / math.sqrt(rows * lax.axis_size("fsdp") * lax.axis_size("rep")), width)

    def swap(a, mask):
        return lax.ppermute(a, "fsdp", [(f, f ^ mask) for f in range(8)])

    other_weight = swap(out_weight, 1)

    there = other_quarter(blocks, segment_ids, out_grad)
    order.mark(there)
    arrived_extra = swap(there, 1)

    ids, rows_held, arrived = order(segment_ids, out_grad, arrived_extra)
    shape = (short + cut, part_width)
    to_send = whole(
        gather_start_kernel, [shape] * (2 * PARTS), rows_held, arrived, scalars=(blocks, ids), name="gather_start"
    )
    order.mark(*to_send)
    gather = {}

    def gather_start(part):
        to_x, to_y = order(*to_send[2 * part : 2 * part + 2])
        gather[part] = to_x, to_y, swap(to_x, 2), swap(to_y, 4)

    def gather_forward(part, *also):
        to_x, to_y, from_x, from_y, *also = order(*gather[part], *also)
        shape = (quarter + cut, part_width)
        next_y, next_x = whole(
            gather_forward_kernel, [shape] * 2, to_x, to_y, from_x, from_y, name="gather_forward"
        )
        order.mark(next_y, next_x, *also)
        gather[part] = to_x, from_x, from_y, next_y, next_x, swap(next_y, 4), swap(next_x, 2)
        return also

    def gather_end(part):
        held = order(*gather[part])
        (plane,) = whole(gather_end_kernel, [(4 * short + quarter, part_width)], *held, name="gather_end")
        order.mark(plane)
        return plane

    def grad_step(part, plane, before):
        held = order(plane, out_weight, other_weight, *before)
        share = grad_part(part, *held[:3], held[3:])
        order.mark(*share)
        return share

    def term_other(plane, attended):
        plane, attended = order(plane, attended)
        shape = (BLOCK, part_width // 2)
        share = whole(term_other_kernel, [shape] * 2, attended, plane, name="term_other")
        order.mark(*share)
        return [swap(half, 1) for half in share]

    def term_own(plane, attended, arrived, pieces=1):
        held = order(attended, plane, *arrived)
        shape = (BLOCK, part_width // pieces)
        total = whole(term_own_kernel, [shape] * pieces, *held, name="term_own")
        order.mark(*total)
        return total

    def attend(half):
        held = order(segment_ids, query_rows, key_rows, value_rows)
        attended, there, weights = forward(blocks[4 * half : 4 * half + 4], *held)
        order.mark(attended, there)
        return attended, weights, swap(there, 1)

    def pack(attended, arrived):
        attended, arrived = order(attended, arrived)
        shape = (short + quarter, PAIR)
        packed = whole(pack_kernel, [shape] * 2, attended, arrived, scalars=(blocks,), name="pack")
        order.mark(*packed)
        return packed

    gather_start(0)
    near, weights_near, near_arriving = attend(0)
    far, weights_far, far_arriving = attend(1)
    (other_weight,) = gather_forward(0, other_weight)

    kept, to_x = pack(near, near_arriving)
    from_x = swap(to_x, 2)
    to_y, to_far = pack(far, far_arriving)
    arriving = from_x, swap(to_y, 4), swap(to_far, 6)
    plane = gather_end(0)
    held = order(kept, *arriving)
    (gathered,) = whole(collect_kernel, [(4 * short + quarter, PAIR)], *held, name="collect")
    order.mark(gathered)

    arriving = term_other(plane, gathered)
    gather_start(1)
    line.start(0, *term_own(plane, gathered, arriving))
    grad = grad_step(0, plane, ())
    gather_forward(1)
    plane = gather_end(1)
    arriving = term_other(plane, gathered)
    gather_start(2)
    grad = grad_step(1, plane, grad)
    line.across(0)
    line.start(1, *term_own(plane, gathered, arriving))
    gather_forward(2)
    plane = gather_end(2)
    arriving = term_other(plane, gathered)
    piece = grad_step(2, plane, grad)
    moved_x, moved_y = swap(piece[1], 2), swap(piece[2], 4)
    line.back(0)
    line.across(1)
    last = term_own(plane, gathered, arriving, 2)
    line.start(2, last[0])

    own, moved_x, moved_y = order(piece[0], moved_x, moved_y)
    tails = jnp.concatenate([own[short:], moved_x[short:], moved_y[short:]], axis=1)
    order.mark(tails)
    line.start(3, order(last[1]))
    there = swap(tails, 1)
    moved_far = swap(order(piece[3]), 6)
    grads = ()

    def finish(i, grad, there, skip):
        weights = weights_near if i < 2 else weights_far
        held = order(grad, there, query_rows, key_rows, value_rows, weights)
        result = backward(blocks[2 * i : 2 * i + 2], held[0], held[1], 1, skip, *held[2:], 2 * (i % 2), grads)
        order.mark(*result)
        return tuple(result)

    grads = finish(0, own, there, 0)
    line.across(2)
    grads = finish(1, moved_x, there, 2)
    line.back(1)
    line.across(3)
    line.finish(0, 0)
    moved_far = order(moved_far)
    tail = moved_far[short:]
    order.mark(tail)
    far_there = swap(tail, 1)
    grads = finish(2, moved_y, there, 4)
    line.back(2)
    grads = finish(3, moved_far, far_there, 0)
    line.back(3)
    line.finish(1, part_width)
    line.finish(2, 2 * part_width)
    line.finish(3, 2 * part_width + part_width // 2)
    return (*grads, *line.done)


def general(query_rows, key_rows, value_rows, out_grad, out_weight, segment_ids):
    rows, width = query_rows.shape
    short = rows // 2
    count = lax.axis_size("fsdp")
    order = jnp.arange(width // BLOCK, dtype=jnp.int32)
    extra = jnp.where((segment_ids[short:] >= 0)[:, None], out_grad[short:], jnp.zeros((), BF16))
    attended, _, weights = forward(order, segment_ids, query_rows, key_rows, value_rows)
    live = jnp.concatenate(
        [lax.all_gather(out_grad[:short], "fsdp", axis=0, tiled=True), lax.psum(extra, "fsdp")]
    )
    attended_live = jnp.concatenate(
        [
            lax.all_to_all(attended[:short], "fsdp", split_axis=1, concat_axis=0, tiled=True),
            lax.psum_scatter(attended[short:], "fsdp", scatter_dimension=1, tiled=True),
        ]
    )
    term = dot(attended_live, live, 0, 0).astype(BF16)
    total = lax.psum(term, "rep").astype(F32)
    grad = dot(live, out_weight, 1, 1).astype(BF16)
    grad_main = lax.all_to_all(
        grad[: count * short], "fsdp", split_axis=0, concat_axis=1, tiled=True
    )
    grad_extra = lax.all_gather(grad[count * short :], "fsdp", axis=1, tiled=True)
    half = short // 2
    grad = jnp.concatenate([grad_main, grad_extra[:half]])
    there = grad_extra[half:]
    grads = backward(order, grad, there, 0, 0, query_rows, key_rows, value_rows, weights, 0, ())
    return (*grads, total * (1.0 / math.sqrt(rows * count * lax.axis_size("rep"))))


def solution(mesh):
    fits = mesh.shape["fsdp"] == 8 and mesh.shape["rep"] == 4
    split = P(("rep", "fsdp"), None)
    return jax.shard_map(
        pairwise if fits else general,
        mesh=mesh,
        in_specs=(split, split, split, split, P("fsdp", None), P(("rep", "fsdp"))),
        out_specs=(split, split, split, P("fsdp", None)),
        check_vma=False,
    )
```

```python
import functools
import math

import jax
import jax.numpy as jnp
from jax import lax
from jax.experimental import pallas as pl
from jax.experimental.pallas import tpu as pltpu
from jax.sharding import PartitionSpec as P

E = 128
BLOCK_HEADS = 3
BLOCK = BLOCK_HEADS * E
PAIR = 2 * BLOCK
PARTS = 2
SHARES = 3
F32 = jnp.float32
BF16 = jnp.bfloat16
LOG2_E = math.log2(math.e)
FAR = -1e30
VMEM_LIMIT = 24 * 1024 * 1024
ATTENTION_VMEM_LIMIT = 40 * 1024 * 1024
NO_COST = pl.CostEstimate(flops=0, bytes_accessed=0, transcendentals=0)


def dot(a, b, a_dim, b_dim):
    return lax.dot_general(a, b, (((a_dim,), (b_dim,)), ((), ())), preferred_element_type=F32)


def forward_kernel(order, ids_column, ids_row, query, key, value, attended, there, weights, bias):
    @pl.when(pl.program_id(0) == 0)
    def _():
        allowed = (ids_column[...] == ids_row[...]) & (ids_column[...] >= 0)
        bias[...] = jnp.where(allowed, 0.0, FAR)

    scale = LOG2_E / math.sqrt(E)
    columns = [slice(head * E, (head + 1) * E) for head in range(BLOCK_HEADS)]
    logits = [dot(key[:, c], query[:, c], 1, 1) * scale + bias[...] for c in columns]
    halves = []
    for head in range(BLOCK_HEADS):
        top = jnp.maximum(jnp.max(logits[head], axis=0, keepdims=True), 0.5 * FAR)
        raw = jnp.exp2(logits[head] - top)
        total = jnp.sum(raw, axis=0, keepdims=True)
        half = (raw * (1.0 / jnp.maximum(total, 0.5))).astype(BF16)
        weights[head] = half
        halves.append(half)
    for head in range(BLOCK_HEADS):
        attended[:, columns[head]] = dot(halves[head], value[:, columns[head]], 0, 0).astype(BF16)
    quarter = there.shape[0]
    start = pl.multiple_of((3 - order[0] % 2) * quarter, 32)
    there[...] = attended[pl.ds(start, quarter), :]


def forward(order, segment_ids, query_rows, key_rows, value_rows):
    rows = query_rows.shape[0]
    blocks = order.shape[0]
    heads = blocks * BLOCK_HEADS
    absolute = pl.BlockSpec((rows, BLOCK), lambda j, order: (0, order[j]))
    return pl.pallas_call(
        forward_kernel,
        grid_spec=pltpu.PrefetchScalarGridSpec(
            num_scalar_prefetch=1,
            grid=(blocks,),
            in_specs=[
                pl.BlockSpec((rows, 1), lambda j, order: (0, 0)),
                pl.BlockSpec((1, rows), lambda j, order: (0, 0)),
                absolute,
                absolute,
                absolute,
            ],
            out_specs=[
                pl.BlockSpec((rows, BLOCK), lambda j, order: (0, j)),
                pl.BlockSpec((rows // 4, BLOCK), lambda j, order: (0, j ^ 1)),
                pl.BlockSpec((BLOCK_HEADS, rows, rows), lambda j, order: (j, 0, 0)),
            ],
            scratch_shapes=[pltpu.VMEM((rows, rows), F32)],
        ),
        out_shape=[
            jax.ShapeDtypeStruct((rows, blocks * BLOCK), BF16),
            jax.ShapeDtypeStruct((rows // 4, blocks * BLOCK), BF16),
            jax.ShapeDtypeStruct((heads, rows, rows), BF16),
        ],
        compiler_params=pltpu.CompilerParams(vmem_limit_bytes=ATTENTION_VMEM_LIMIT),
        cost_estimate=NO_COST,
        name="attention_forward",
    )(order, segment_ids.reshape(rows, 1), segment_ids.reshape(1, rows), query_rows, key_rows, value_rows)


def backward_kernel(order, grad_main, grad_here, grad_there, query, key, value, weights, *rest):
    grad_query, grad_key, grad_value = rest[-3:]
    first = order[0] % 2 == 0
    here, there = grad_here[...], grad_there[...]
    grad_all = jnp.concatenate(
        [grad_main[...], jnp.where(first, here, there), jnp.where(first, there, here)], axis=0
    )
    inverse_root = 1.0 / math.sqrt(E)
    for head in range(BLOCK_HEADS):
        columns = slice(head * E, (head + 1) * E)
        grad = grad_all[:, columns]
        half = weights[head]
        grad_probs = dot(value[:, columns], grad, 1, 1)
        wide = half.astype(F32)
        row_dot = jnp.sum(wide * grad_probs, axis=0, keepdims=True)
        grad_logits = (wide * (grad_probs - row_dot)).astype(BF16)
        grad_value[:, columns] = dot(half, grad, 1, 0).astype(BF16)
        grad_key[:, columns] = (dot(grad_logits, query[:, columns], 1, 0) * inverse_root).astype(BF16)
        grad_query[:, columns] = (dot(grad_logits, key[:, columns], 0, 0) * inverse_root).astype(BF16)


def backward(order, grad, there, flip, there_skip, query_rows, key_rows, value_rows, weights, skip, done):
    rows, width = query_rows.shape
    quarter = there.shape[0]
    blocks = order.shape[0]
    heads = blocks * BLOCK_HEADS
    absolute = pl.BlockSpec((rows, BLOCK), lambda j, order: (0, order[j]))
    shapes = [jax.ShapeDtypeStruct((rows, width), BF16)] * 3
    return pl.pallas_call(
        backward_kernel,
        grid_spec=pltpu.PrefetchScalarGridSpec(
            num_scalar_prefetch=1,
            grid=(blocks,),
            in_specs=[
                pl.BlockSpec((2 * quarter, BLOCK), lambda j, order: (0, j)),
                pl.BlockSpec((quarter, BLOCK), lambda j, order: (2, j)),
                pl.BlockSpec((quarter, BLOCK), lambda j, order: (0, (j ^ flip) + there_skip)),
                absolute,
                absolute,
                absolute,
                pl.BlockSpec((BLOCK_HEADS, rows, rows), lambda j, order: (j + skip, 0, 0)),
            ]
            + [pl.BlockSpec(memory_space=pl.ANY)] * len(done),
            out_specs=[absolute, absolute, absolute],
        ),
        out_shape=shapes,
        input_output_aliases={8 + i: i for i in range(len(done))},
        compiler_params=pltpu.CompilerParams(vmem_limit_bytes=ATTENTION_VMEM_LIMIT),
        cost_estimate=NO_COST,
        name="attention_backward",
    )(order, grad, grad, there, query_rows, key_rows, value_rows, weights, *done)


def whole(kernel, shapes, *arrays, scalars=(), name):
    vmem, smem = pl.BlockSpec(memory_space=pltpu.VMEM), pl.BlockSpec(memory_space=pltpu.SMEM)
    return pl.pallas_call(
        kernel,
        in_specs=[smem] * len(scalars) + [vmem] * len(arrays),
        out_specs=[vmem] * len(shapes),
        out_shape=[jax.ShapeDtypeStruct(shape, BF16) for shape in shapes],
        compiler_params=pltpu.CompilerParams(vmem_limit_bytes=VMEM_LIMIT),
        cost_estimate=NO_COST,
        name=name,
    )(*scalars, *arrays)


def other_quarter_kernel(blocks, ids, extra, out):
    is_full = ids[ids.shape[0] - 1] >= 0
    out[...] = jnp.where(is_full, extra[...], jnp.zeros((), BF16))


def other_quarter(blocks, ids, rows):
    count, width = rows.shape
    quarter = count // 4
    return pl.pallas_call(
        other_quarter_kernel,
        grid_spec=pltpu.PrefetchScalarGridSpec(
            num_scalar_prefetch=2,
            grid=(1,),
            in_specs=[pl.BlockSpec((quarter, width), lambda i, blocks, ids: (3 - blocks[0] % 2, 0))],
            out_specs=pl.BlockSpec((quarter, width), lambda i, blocks, ids: (0, 0)),
        ),
        out_shape=jax.ShapeDtypeStruct((quarter, width), BF16),
        compiler_params=pltpu.CompilerParams(vmem_limit_bytes=ATTENTION_VMEM_LIMIT),
        cost_estimate=NO_COST,
        name="other_quarter",
    )(blocks, ids, rows)


def gather_start_kernel(blocks, ids, rows, arrived, *outs):
    quarter = arrived.shape[0]
    short, cut = 2 * quarter, quarter // 2
    is_full = ids[ids.shape[0] - 1] >= 0
    start = pl.multiple_of(short + quarter * (blocks[0] % 2), 32)
    own = jnp.where(is_full, rows[pl.ds(start, quarter), :], jnp.zeros((), BF16))
    here = own + arrived[...]
    width = outs[0].shape[1]
    for part in range(len(outs) // 2):
        columns = slice(part * width, (part + 1) * width)
        for i in range(2):
            outs[2 * part + i][:short] = rows[:short, columns]
            outs[2 * part + i][short:] = here[i * cut : (i + 1) * cut, columns]


def gather_forward_kernel(to_x, to_y, from_x, from_y, next_y, next_x):
    quarter = from_x.shape[0] * 2 // 5
    short = 2 * quarter
    next_y[:quarter] = from_x[:quarter]
    next_x[:quarter] = from_y[quarter:short]
    next_y[quarter:] = to_x[short:] + from_x[short:]
    next_x[quarter:] = to_y[short:] + from_y[short:]


def gather_end_kernel(to_x, from_x, from_y, next_y, next_x, via_y, via_x, plane):
    quarter = to_x.shape[0] * 2 // 5
    short, cut = 2 * quarter, quarter // 2
    plane[:short] = to_x[:short]
    plane[short : 2 * short] = from_x[:short]
    plane[2 * short : 3 * short] = from_y[:short]
    plane[3 * short : 3 * short + quarter] = via_y[:quarter]
    plane[3 * short + quarter : 4 * short] = via_x[:quarter]
    plane[4 * short : 4 * short + cut] = next_y[quarter:] + via_y[quarter:]
    plane[4 * short + cut :] = next_x[quarter:] + via_x[quarter:]


def pack_kernel(blocks, attended, arrived, *outs):
    quarter = arrived.shape[0]
    short = 2 * quarter
    start = pl.multiple_of(short + quarter * (blocks[0] % 2), 32)
    extra = attended[pl.ds(start, quarter), :] + arrived[...]
    for i, out in enumerate(outs):
        columns = slice(i * PAIR, (i + 1) * PAIR)
        out[:short] = attended[:short, columns]
        out[short:] = extra[:, columns]


def collect_kernel(kept, from_x, from_y, from_far, gathered):
    short = kept.shape[0] * 2 // 3
    parts = [kept, from_x, from_y, from_far]
    for i, part in enumerate(parts):
        gathered[i * short : (i + 1) * short] = part[:short]
    gathered[4 * short :] = (kept[short:] + from_x[short:]) + (from_y[short:] + from_far[short:])


def term_other_kernel(attended, plane, *outs):
    share = dot(attended[:, BLOCK:], plane[...], 0, 0).astype(BF16)
    width = share.shape[1] // len(outs)
    for i, out in enumerate(outs):
        out[...] = share[:, i * width : (i + 1) * width]


def term_own_kernel(attended, plane, *refs):
    arrived, outs = refs[:-2], refs[-2:]
    own = dot(attended[:, :BLOCK], plane[...], 0, 0)
    there = jnp.concatenate([a[...] for a in arrived], axis=1)
    total = (own + there.astype(F32)).astype(BF16)
    width = outs[0].shape[1]
    for i, out in enumerate(outs):
        out[...] = total[:, i * width : (i + 1) * width]


def grad_kernel(plane, own, other, *rest):
    for i, weight in enumerate((own, other)):
        columns = slice(i * BLOCK, (i + 1) * BLOCK)
        share = dot(plane[...], weight[...], 1, 1)
        if len(rest) == 2:
            share = rest[0][:, columns] + share
        rest[-1][:, columns] = share


def grad_end_kernel(plane, own, other, before, *pieces):
    rows = pieces[0].shape[0]
    short = rows * 2 // 3
    for i, weight in enumerate((own, other)):
        columns = slice(i * BLOCK, (i + 1) * BLOCK)
        total = (before[:, columns] + dot(plane[...], weight[...], 1, 1)).astype(BF16)
        for j, piece in enumerate(pieces[:-1]):
            piece[:short, columns] = total[j * short : (j + 1) * short]
            piece[short:, columns] = total[4 * short :]
        pieces[-1][:, columns] = total[4 * short :]


def grad_part(part, plane, own_weight, other_weight, before):
    count, width = plane.shape
    weight = pl.BlockSpec((BLOCK, width), lambda i: (0, part))
    result = pl.BlockSpec((count, PAIR), lambda i: (0, 0))
    last = part == PARTS - 1
    rows = count // 3
    piece = pl.BlockSpec((rows, PAIR), lambda i: (0, 0))
    return pl.pallas_call(
        grad_end_kernel if last else grad_kernel,
        grid=(1,),
        in_specs=[pl.BlockSpec((count, width), lambda i: (0, 0)), weight, weight] + [result] * len(before),
        out_specs=[piece] * 4 + [pl.BlockSpec((rows // 3, PAIR), lambda i: (0, 0))] if last else [result],
        out_shape=[jax.ShapeDtypeStruct((rows, PAIR), BF16)] * 4 + [jax.ShapeDtypeStruct((rows // 3, PAIR), BF16)]
        if last
        else [jax.ShapeDtypeStruct((count, PAIR), F32)],
        compiler_params=pltpu.CompilerParams(vmem_limit_bytes=VMEM_LIMIT),
        cost_estimate=NO_COST,
        name="grad_attended",
    )(plane, own_weight, other_weight, *before)


def add_kernel(a, b, out):
    out[...] = (a[...].astype(F32) + b[...].astype(F32)).astype(BF16)


class Order:
    def __init__(self):
        self.last = ()

    def __call__(self, *arrays):
        held = lax.optimization_barrier((*self.last, *arrays))[len(self.last) :]
        return held[0] if len(held) == 1 else held

    def mark(self, *arrays):
        self.last = tuple(arrays)


def add(a, b):
    return whole(add_kernel, [a.shape], a, b, name="add")[0]


def line_end_kernel(scale, place, total, arrived, *rest):
    in_middle = (place[0] == 1) | (place[0] == 2)
    rest[-1][...] = jnp.where(in_middle, total[...], arrived[...]).astype(F32) * scale


def line_end(scale, place, total, arrived, start, all_width, done):
    rows, width = total.shape
    piece = pl.BlockSpec((rows, width), lambda i, place: (0, 0))
    return pl.pallas_call(
        functools.partial(line_end_kernel, scale),
        grid_spec=pltpu.PrefetchScalarGridSpec(
            num_scalar_prefetch=1,
            grid=(1,),
            in_specs=[piece, piece] + [pl.BlockSpec(memory_space=pl.ANY)] * len(done),
            out_specs=pl.BlockSpec((rows, width), lambda i, place: (0, start // width)),
        ),
        out_shape=jax.ShapeDtypeStruct((rows, all_width), F32),
        input_output_aliases={3 + i: i for i in range(len(done))},
        compiler_params=pltpu.CompilerParams(vmem_limit_bytes=VMEM_LIMIT),
        cost_estimate=NO_COST,
        name="line_end",
    )(place, total, arrived, *done)


class LineSum:
    def __init__(self, order, scale, width):
        self.order, self.scale, self.width = order, scale, width
        self.place = lax.axis_index("rep").astype(jnp.int32).reshape(1)
        self.held, self.arriving, self.done = {}, {}, ()

    def start(self, piece, part):
        self.held[piece] = part
        self.arriving[piece] = lax.ppermute(part, "rep", [(0, 1), (3, 2)])

    def across(self, piece):
        part, arrived = self.order(self.held[piece], self.arriving[piece])
        pair = add(part, arrived)
        self.order.mark(pair)
        self.held[piece] = pair
        self.arriving[piece] = lax.ppermute(pair, "rep", [(1, 2), (2, 1)])

    def back(self, piece):
        pair, arrived = self.order(self.held[piece], self.arriving[piece])
        total = add(pair, arrived)
        self.order.mark(total)
        self.held[piece] = total
        self.arriving[piece] = lax.ppermute(total, "rep", [(1, 0), (2, 3)])

    def finish(self, piece, start):
        held = self.order(self.held[piece], self.arriving[piece], *self.done)
        result = line_end(self.scale, self.place, held[0], held[1], start, self.width, held[2:])
        self.order.mark(result)
        self.done = (result,)


def pairwise(query_rows, key_rows, value_rows, out_grad, out_weight, segment_ids):
    rows, width = query_rows.shape
    short = rows // 2
    quarter = short // 2
    cut = quarter // 2
    part_width = width // PARTS
    me = lax.axis_index("fsdp")
    core = me % 2
    blocks = me ^ jnp.arange(8, dtype=jnp.int32)
    order = Order()
    line = LineSum(order, 1.0 / math.sqrt(rows * lax.axis_size("fsdp") * lax.axis_size("rep")), width)

    def swap(a, mask):
        return lax.ppermute(a, "fsdp", [(f, f ^ mask) for f in range(8)])

    other_weight = swap(out_weight, 1)

    there = other_quarter(blocks, segment_ids, out_grad)
    order.mark(there)
    arrived_extra = swap(there, 1)

    ids, rows_held, arrived = order(segment_ids, out_grad, arrived_extra)
    shape = (short + cut, part_width)
    to_send = whole(
        gather_start_kernel, [shape] * (2 * PARTS), rows_held, arrived, scalars=(blocks, ids), name="gather_start"
    )
    order.mark(*to_send)
    gather = {}

    def gather_start(part):
        to_x, to_y = order(*to_send[2 * part : 2 * part + 2])
        gather[part] = to_x, to_y, swap(to_x, 2), swap(to_y, 4)

    def gather_forward(part, *also):
        to_x, to_y, from_x, from_y, *also = order(*gather[part], *also)
        shape = (quarter + cut, part_width)
        next_y, next_x = whole(
            gather_forward_kernel, [shape] * 2, to_x, to_y, from_x, from_y, name="gather_forward"
        )
        order.mark(next_y, next_x, *also)
        gather[part] = to_x, from_x, from_y, next_y, next_x, swap(next_y, 4), swap(next_x, 2)
        return also

    def gather_end(part):
        held = order(*gather[part])
        (plane,) = whole(gather_end_kernel, [(4 * short + quarter, part_width)], *held, name="gather_end")
        order.mark(plane)
        return plane

    def grad_step(part, plane, before):
        held = order(plane, out_weight, other_weight, *before)
        share = grad_part(part, *held[:3], held[3:])
        order.mark(*share)
        return share

    def term_other(plane, attended):
        plane, attended = order(plane, attended)
        shape = (BLOCK, part_width // SHARES)
        share = whole(term_other_kernel, [shape] * SHARES, attended, plane, name="term_other")
        order.mark(*share)
        return [swap(piece, 1) for piece in share]

    def term_own(plane, attended, arrived):
        held = order(attended, plane, *arrived)
        pieces = whole(term_own_kernel, [(BLOCK, part_width // 2)] * 2, *held, name="term_own")
        order.mark(*pieces)
        return pieces

    def attend(half):
        held = order(segment_ids, query_rows, key_rows, value_rows)
        attended, there, weights = forward(blocks[4 * half : 4 * half + 4], *held)
        order.mark(attended, there)
        return attended, weights, swap(there, 1)

    def pack(attended, arrived):
        attended, arrived = order(attended, arrived)
        shape = (short + quarter, PAIR)
        packed = whole(pack_kernel, [shape] * 2, attended, arrived, scalars=(blocks,), name="pack")
        order.mark(*packed)
        return packed

    gather_start(0)
    near, weights_near, near_arriving = attend(0)
    far, weights_far, far_arriving = attend(1)
    (other_weight,) = gather_forward(0, other_weight)

    kept, to_x = pack(near, near_arriving)
    from_x = swap(to_x, 2)
    to_y, to_far = pack(far, far_arriving)
    arriving = from_x, swap(to_y, 4), swap(to_far, 6)
    plane = gather_end(0)
    grad = grad_step(0, plane, ())
    held = order(kept, *arriving)
    (gathered,) = whole(collect_kernel, [(4 * short + quarter, PAIR)], *held, name="collect")
    order.mark(gathered)

    arriving = term_other(plane, gathered)
    gather_start(1)
    pieces = term_own(plane, gathered, arriving)
    line.start(0, pieces[0])
    line.start(1, pieces[1])
    gather_forward(1)
    line.across(0)
    plane = gather_end(1)
    arriving = term_other(plane, gathered)
    line.across(1)
    pieces = term_own(plane, gathered, arriving)
    line.start(2, pieces[0])
    line.back(0)
    line.start(3, order(pieces[1]))
    *piece, own_tail = grad_step(1, plane, grad)
    moved_x, moved_y = swap(piece[1], 2), swap(piece[2], 4)
    line.back(1)
    line.across(2)
    line.finish(0, 0)

    own_tail, moved_x, moved_y = order(own_tail, moved_x, moved_y)
    tails = [own_tail, moved_x[short:], moved_y[short:]]
    order.mark(*tails)
    there = [swap(tail, 1) for tail in tails]
    moved_far = swap(order(piece[3]), 6)
    grads = ()

    def finish(i, grad, there):
        weights = weights_near if i < 2 else weights_far
        held = order(grad, there, query_rows, key_rows, value_rows, weights)
        result = backward(blocks[2 * i : 2 * i + 2], held[0], held[1], 1, 0, *held[2:], 2 * (i % 2), grads)
        order.mark(*result)
        return tuple(result)

    grads = finish(0, piece[0], there[0])
    line.across(3)
    line.back(2)
    line.finish(1, part_width // 2)
    grads = finish(1, moved_x, there[1])
    moved_far = order(moved_far)
    tail = moved_far[short:]
    order.mark(tail)
    far_there = swap(tail, 1)
    line.back(3)
    grads = finish(2, moved_y, there[2])
    line.finish(2, part_width)
    grads = finish(3, moved_far, far_there)
    line.finish(3, part_width + part_width // 2)
    return (*grads, *line.done)


def general(query_rows, key_rows, value_rows, out_grad, out_weight, segment_ids):
    rows, width = query_rows.shape
    short = rows // 2
    count = lax.axis_size("fsdp")
    order = jnp.arange(width // BLOCK, dtype=jnp.int32)
    extra = jnp.where((segment_ids[short:] >= 0)[:, None], out_grad[short:], jnp.zeros((), BF16))
    attended, _, weights = forward(order, segment_ids, query_rows, key_rows, value_rows)
    live = jnp.concatenate(
        [lax.all_gather(out_grad[:short], "fsdp", axis=0, tiled=True), lax.psum(extra, "fsdp")]
    )
    attended_live = jnp.concatenate(
        [
            lax.all_to_all(attended[:short], "fsdp", split_axis=1, concat_axis=0, tiled=True),
            lax.psum_scatter(attended[short:], "fsdp", scatter_dimension=1, tiled=True),
        ]
    )
    term = dot(attended_live, live, 0, 0).astype(BF16)
    total = lax.psum(term, "rep").astype(F32)
    grad = dot(live, out_weight, 1, 1).astype(BF16)
    grad_main = lax.all_to_all(
        grad[: count * short], "fsdp", split_axis=0, concat_axis=1, tiled=True
    )
    grad_extra = lax.all_gather(grad[count * short :], "fsdp", axis=1, tiled=True)
    half = short // 2
    grad = jnp.concatenate([grad_main, grad_extra[:half]])
    there = grad_extra[half:]
    grads = backward(order, grad, there, 0, 0, query_rows, key_rows, value_rows, weights, 0, ())
    return (*grads, total * (1.0 / math.sqrt(rows * count * lax.axis_size("rep"))))


def solution(mesh):
    fits = mesh.shape["fsdp"] == 8 and mesh.shape["rep"] == 4
    split = P(("rep", "fsdp"), None)
    return jax.shard_map(
        pairwise if fits else general,
        mesh=mesh,
        in_specs=(split, split, split, split, P("fsdp", None), P(("rep", "fsdp"))),
        out_specs=(split, split, split, P("fsdp", None)),
        check_vma=False,
    )
```

```python
import functools
import math

import jax
import jax.numpy as jnp
from jax import lax
from jax.experimental import pallas as pl
from jax.experimental.pallas import tpu as pltpu
from jax.sharding import PartitionSpec as P

E = 128
BLOCK_HEADS = 3
BLOCK = BLOCK_HEADS * E
PAIR = 2 * BLOCK
PARTS = 2
SHARES = 3
F32 = jnp.float32
BF16 = jnp.bfloat16
LOG2_E = math.log2(math.e)
FAR = -1e30
VMEM_LIMIT = 24 * 1024 * 1024
ATTENTION_VMEM_LIMIT = 40 * 1024 * 1024
NO_COST = pl.CostEstimate(flops=0, bytes_accessed=0, transcendentals=0)


def dot(a, b, a_dim, b_dim):
    return lax.dot_general(a, b, (((a_dim,), (b_dim,)), ((), ())), preferred_element_type=F32)


def forward_kernel(order, ids_column, ids_row, query, key, value, attended, there, weights, bias):
    @pl.when(pl.program_id(0) == 0)
    def _():
        allowed = (ids_column[...] == ids_row[...]) & (ids_column[...] >= 0)
        bias[...] = jnp.where(allowed, 0.0, FAR)

    scale = LOG2_E / math.sqrt(E)
    columns = [slice(head * E, (head + 1) * E) for head in range(BLOCK_HEADS)]
    logits = [dot(key[:, c], query[:, c], 1, 1) * scale + bias[...] for c in columns]
    halves = []
    for head in range(BLOCK_HEADS):
        top = jnp.maximum(jnp.max(logits[head], axis=0, keepdims=True), 0.5 * FAR)
        raw = jnp.exp2(logits[head] - top)
        total = jnp.sum(raw, axis=0, keepdims=True)
        half = (raw * (1.0 / jnp.maximum(total, 0.5))).astype(BF16)
        weights[head] = half
        halves.append(half)
    for head in range(BLOCK_HEADS):
        attended[:, columns[head]] = dot(halves[head], value[:, columns[head]], 0, 0).astype(BF16)
    quarter = there.shape[0]
    start = pl.multiple_of((3 - order[0] % 2) * quarter, 32)
    there[...] = attended[pl.ds(start, quarter), :]


def forward(order, segment_ids, query_rows, key_rows, value_rows):
    rows = query_rows.shape[0]
    blocks = order.shape[0]
    heads = blocks * BLOCK_HEADS
    absolute = pl.BlockSpec((rows, BLOCK), lambda j, order: (0, order[j]))
    return pl.pallas_call(
        forward_kernel,
        grid_spec=pltpu.PrefetchScalarGridSpec(
            num_scalar_prefetch=1,
            grid=(blocks,),
            in_specs=[
                pl.BlockSpec((rows, 1), lambda j, order: (0, 0)),
                pl.BlockSpec((1, rows), lambda j, order: (0, 0)),
                absolute,
                absolute,
                absolute,
            ],
            out_specs=[
                pl.BlockSpec((rows, BLOCK), lambda j, order: (0, j)),
                pl.BlockSpec((rows // 4, BLOCK), lambda j, order: (0, j ^ 1)),
                pl.BlockSpec((BLOCK_HEADS, rows, rows), lambda j, order: (j, 0, 0)),
            ],
            scratch_shapes=[pltpu.VMEM((rows, rows), F32)],
        ),
        out_shape=[
            jax.ShapeDtypeStruct((rows, blocks * BLOCK), BF16),
            jax.ShapeDtypeStruct((rows // 4, blocks * BLOCK), BF16),
            jax.ShapeDtypeStruct((heads, rows, rows), BF16),
        ],
        compiler_params=pltpu.CompilerParams(vmem_limit_bytes=ATTENTION_VMEM_LIMIT),
        cost_estimate=NO_COST,
        name="attention_forward",
    )(order, segment_ids.reshape(rows, 1), segment_ids.reshape(1, rows), query_rows, key_rows, value_rows)


def backward_kernel(order, grad_rows, query, key, value, weights, *rest):
    grad_query, grad_key, grad_value = rest[-3:]
    inverse_root = 1.0 / math.sqrt(E)
    for head in range(BLOCK_HEADS):
        columns = slice(head * E, (head + 1) * E)
        grad = grad_rows[:, columns]
        half = weights[head]
        grad_probs = dot(value[:, columns], grad, 1, 1)
        wide = half.astype(F32)
        row_dot = jnp.sum(wide * grad_probs, axis=0, keepdims=True)
        grad_logits = (wide * (grad_probs - row_dot)).astype(BF16)
        grad_value[:, columns] = dot(half, grad, 1, 0).astype(BF16)
        grad_key[:, columns] = (dot(grad_logits, query[:, columns], 1, 0) * inverse_root).astype(BF16)
        grad_query[:, columns] = (dot(grad_logits, key[:, columns], 0, 0) * inverse_root).astype(BF16)


def backward(order, grad, query_rows, key_rows, value_rows, weights, skip, done):
    rows, width = query_rows.shape
    blocks = order.shape[0]
    heads = blocks * BLOCK_HEADS
    absolute = pl.BlockSpec((rows, BLOCK), lambda j, order: (0, order[j]))
    shapes = [jax.ShapeDtypeStruct((rows, width), BF16)] * 3
    return pl.pallas_call(
        backward_kernel,
        grid_spec=pltpu.PrefetchScalarGridSpec(
            num_scalar_prefetch=1,
            grid=(blocks,),
            in_specs=[
                pl.BlockSpec((rows, BLOCK), lambda j, order: (0, j)),
                absolute,
                absolute,
                absolute,
                pl.BlockSpec((BLOCK_HEADS, rows, rows), lambda j, order: (j + skip, 0, 0)),
            ]
            + [pl.BlockSpec(memory_space=pl.ANY)] * len(done),
            out_specs=[absolute, absolute, absolute],
        ),
        out_shape=shapes,
        input_output_aliases={6 + i: i for i in range(len(done))},
        compiler_params=pltpu.CompilerParams(vmem_limit_bytes=ATTENTION_VMEM_LIMIT),
        cost_estimate=NO_COST,
        name="attention_backward",
    )(order, grad, query_rows, key_rows, value_rows, weights, *done)


def whole(kernel, shapes, *arrays, scalars=(), name):
    vmem, smem = pl.BlockSpec(memory_space=pltpu.VMEM), pl.BlockSpec(memory_space=pltpu.SMEM)
    return pl.pallas_call(
        kernel,
        in_specs=[smem] * len(scalars) + [vmem] * len(arrays),
        out_specs=[vmem] * len(shapes),
        out_shape=[jax.ShapeDtypeStruct(shape, BF16) for shape in shapes],
        compiler_params=pltpu.CompilerParams(vmem_limit_bytes=VMEM_LIMIT),
        cost_estimate=NO_COST,
        name=name,
    )(*scalars, *arrays)


def other_quarter_kernel(blocks, ids, extra, out):
    is_full = ids[ids.shape[0] - 1] >= 0
    out[...] = jnp.where(is_full, extra[...], jnp.zeros((), BF16))


def other_quarter(blocks, ids, rows):
    count, width = rows.shape
    quarter = count // 4
    return pl.pallas_call(
        other_quarter_kernel,
        grid_spec=pltpu.PrefetchScalarGridSpec(
            num_scalar_prefetch=2,
            grid=(1,),
            in_specs=[pl.BlockSpec((quarter, width), lambda i, blocks, ids: (3 - blocks[0] % 2, 0))],
            out_specs=pl.BlockSpec((quarter, width), lambda i, blocks, ids: (0, 0)),
        ),
        out_shape=jax.ShapeDtypeStruct((quarter, width), BF16),
        compiler_params=pltpu.CompilerParams(vmem_limit_bytes=ATTENTION_VMEM_LIMIT),
        cost_estimate=NO_COST,
        name="other_quarter",
    )(blocks, ids, rows)


def gather_start_kernel(blocks, ids, rows, arrived, *outs):
    quarter = arrived.shape[0]
    short, cut = 2 * quarter, quarter // 2
    is_full = ids[ids.shape[0] - 1] >= 0
    start = pl.multiple_of(short + quarter * (blocks[0] % 2), 32)
    own = jnp.where(is_full, rows[pl.ds(start, quarter), :], jnp.zeros((), BF16))
    here = own + arrived[...]
    width = outs[0].shape[1]
    for part in range(len(outs) // 2):
        columns = slice(part * width, (part + 1) * width)
        for i in range(2):
            outs[2 * part + i][:short] = rows[:short, columns]
            outs[2 * part + i][short:] = here[i * cut : (i + 1) * cut, columns]


def gather_forward_kernel(to_x, to_y, from_x, from_y, next_y, next_x):
    quarter = from_x.shape[0] * 2 // 5
    short = 2 * quarter
    next_y[:quarter] = from_x[:quarter]
    next_x[:quarter] = from_y[quarter:short]
    next_y[quarter:] = to_x[short:] + from_x[short:]
    next_x[quarter:] = to_y[short:] + from_y[short:]


def gather_end_kernel(to_x, from_x, from_y, next_y, next_x, via_y, via_x, plane):
    quarter = to_x.shape[0] * 2 // 5
    short, cut = 2 * quarter, quarter // 2
    plane[:short] = to_x[:short]
    plane[short : 2 * short] = from_x[:short]
    plane[2 * short : 3 * short] = from_y[:short]
    plane[3 * short : 3 * short + quarter] = via_y[:quarter]
    plane[3 * short + quarter : 4 * short] = via_x[:quarter]
    plane[4 * short : 4 * short + cut] = next_y[quarter:] + via_y[quarter:]
    plane[4 * short + cut :] = next_x[quarter:] + via_x[quarter:]


def pack_kernel(blocks, attended, arrived, *outs):
    quarter = arrived.shape[0]
    short = 2 * quarter
    start = pl.multiple_of(short + quarter * (blocks[0] % 2), 32)
    extra = attended[pl.ds(start, quarter), :] + arrived[...]
    for i, out in enumerate(outs):
        columns = slice(i * PAIR, (i + 1) * PAIR)
        out[:short] = attended[:short, columns]
        out[short:] = extra[:, columns]


def collect_kernel(kept, from_x, from_y, from_far, gathered):
    short = kept.shape[0] * 2 // 3
    parts = [kept, from_x, from_y, from_far]
    for i, part in enumerate(parts):
        gathered[i * short : (i + 1) * short] = part[:short]
    gathered[4 * short :] = (kept[short:] + from_x[short:]) + (from_y[short:] + from_far[short:])


def term_other_kernel(begin, attended, plane, *outs):
    width = outs[0].shape[1]
    share = dot(attended[:, BLOCK:], plane[:, begin : begin + len(outs) * width], 0, 0).astype(BF16)
    for i, out in enumerate(outs):
        out[...] = share[:, i * width : (i + 1) * width]


def term_own_kernel(begin, attended, plane, *refs):
    arrived, out = refs[:-1], refs[-1]
    own = dot(attended[:, :BLOCK], plane[:, begin : begin + out.shape[1]], 0, 0)
    there = jnp.concatenate([a[...] for a in arrived], axis=1)
    out[...] = (own + there.astype(F32)).astype(BF16)


def grad_kernel(plane, own, other, *rest):
    for i, weight in enumerate((own, other)):
        columns = slice(i * BLOCK, (i + 1) * BLOCK)
        share = dot(plane[...], weight[...], 1, 1)
        if len(rest) == 2:
            share = rest[0][:, columns] + share
        rest[-1][:, columns] = share


def grad_end_kernel(plane, own, other, before, main, extra):
    rows = main.shape[0]
    for i, weight in enumerate((own, other)):
        columns = slice(i * BLOCK, (i + 1) * BLOCK)
        total = (before[:, columns] + dot(plane[...], weight[...], 1, 1)).astype(BF16)
        main[:, columns] = total[:rows]
        extra[:, columns] = total[rows:]


def grad_pack_kernel(blocks, main, extra, arrived, *outs):
    short = main.shape[0] // len(outs)
    quarter = extra.shape[0]
    first = blocks[0] % 2 == 0
    there = jnp.concatenate([arrived[:, BLOCK:], arrived[:, :BLOCK]], axis=1)
    for i, out in enumerate(outs):
        out[:short] = main[i * short : (i + 1) * short]
        out[short : short + quarter] = jnp.where(first, extra[...], there)
        out[short + quarter :] = jnp.where(first, there, extra[...])


def grad_part(part, plane, own_weight, other_weight, before):
    count, width = plane.shape
    weight = pl.BlockSpec((BLOCK, width), lambda i: (0, part))
    result = pl.BlockSpec((count, PAIR), lambda i: (0, 0))
    last = part == PARTS - 1
    extra = count // 9
    outs = [(count - extra, PAIR), (extra, PAIR)]
    return pl.pallas_call(
        grad_end_kernel if last else grad_kernel,
        grid=(1,),
        in_specs=[pl.BlockSpec((count, width), lambda i: (0, 0)), weight, weight] + [result] * len(before),
        out_specs=[pl.BlockSpec(shape, lambda i: (0, 0)) for shape in outs] if last else [result],
        out_shape=[jax.ShapeDtypeStruct(shape, BF16) for shape in outs]
        if last
        else [jax.ShapeDtypeStruct((count, PAIR), F32)],
        compiler_params=pltpu.CompilerParams(vmem_limit_bytes=VMEM_LIMIT),
        cost_estimate=NO_COST,
        name="grad_attended",
    )(plane, own_weight, other_weight, *before)


def add_kernel(a, b, out):
    out[...] = (a[...].astype(F32) + b[...].astype(F32)).astype(BF16)


class Order:
    def __init__(self):
        self.last = ()

    def __call__(self, *arrays):
        held = lax.optimization_barrier((*self.last, *arrays))[len(self.last) :]
        return held[0] if len(held) == 1 else held

    def mark(self, *arrays):
        self.last = tuple(arrays)


def add(a, b):
    return whole(add_kernel, [a.shape], a, b, name="add")[0]


def line_end_kernel(scale, place, total, arrived, *rest):
    in_middle = (place[0] == 1) | (place[0] == 2)
    rest[-1][...] = jnp.where(in_middle, total[...], arrived[...]).astype(F32) * scale


def line_end(scale, place, total, arrived, start, all_width, done):
    rows, width = total.shape
    piece = pl.BlockSpec((rows, width), lambda i, place: (0, 0))
    return pl.pallas_call(
        functools.partial(line_end_kernel, scale),
        grid_spec=pltpu.PrefetchScalarGridSpec(
            num_scalar_prefetch=1,
            grid=(1,),
            in_specs=[piece, piece] + [pl.BlockSpec(memory_space=pl.ANY)] * len(done),
            out_specs=pl.BlockSpec((rows, width), lambda i, place: (0, start // width)),
        ),
        out_shape=jax.ShapeDtypeStruct((rows, all_width), F32),
        input_output_aliases={3 + i: i for i in range(len(done))},
        compiler_params=pltpu.CompilerParams(vmem_limit_bytes=VMEM_LIMIT),
        cost_estimate=NO_COST,
        name="line_end",
    )(place, total, arrived, *done)


class LineSum:
    def __init__(self, order, scale, width):
        self.order, self.scale, self.width = order, scale, width
        self.place = lax.axis_index("rep").astype(jnp.int32).reshape(1)
        self.held, self.arriving, self.done = {}, {}, ()

    def start(self, piece, part):
        self.held[piece] = part
        self.arriving[piece] = lax.ppermute(part, "rep", [(0, 1), (3, 2)])

    def across(self, piece):
        part, arrived = self.order(self.held[piece], self.arriving[piece])
        pair = add(part, arrived)
        self.order.mark(pair)
        self.held[piece] = pair
        self.arriving[piece] = lax.ppermute(pair, "rep", [(1, 2), (2, 1)])

    def back(self, piece):
        pair, arrived = self.order(self.held[piece], self.arriving[piece])
        total = add(pair, arrived)
        self.order.mark(total)
        self.held[piece] = total
        self.arriving[piece] = lax.ppermute(total, "rep", [(1, 0), (2, 3)])

    def finish(self, piece, start):
        held = self.order(self.held[piece], self.arriving[piece], *self.done)
        result = line_end(self.scale, self.place, held[0], held[1], start, self.width, held[2:])
        self.order.mark(result)
        self.done = (result,)


def pairwise(query_rows, key_rows, value_rows, out_grad, out_weight, segment_ids):
    rows, width = query_rows.shape
    short = rows // 2
    quarter = short // 2
    cut = quarter // 2
    part_width = width // PARTS
    me = lax.axis_index("fsdp")
    core = me % 2
    blocks = me ^ jnp.arange(8, dtype=jnp.int32)
    order = Order()
    line = LineSum(order, 1.0 / math.sqrt(rows * lax.axis_size("fsdp") * lax.axis_size("rep")), width)

    def swap(a, mask):
        return lax.ppermute(a, "fsdp", [(f, f ^ mask) for f in range(8)])

    other_weight = swap(out_weight, 1)

    there = other_quarter(blocks, segment_ids, out_grad)
    order.mark(there)
    arrived_extra = swap(there, 1)

    ids, rows_held, arrived = order(segment_ids, out_grad, arrived_extra)
    shape = (short + cut, part_width)
    to_send = whole(
        gather_start_kernel, [shape] * (2 * PARTS), rows_held, arrived, scalars=(blocks, ids), name="gather_start"
    )
    order.mark(*to_send)
    gather = {}

    def gather_start(part):
        to_x, to_y = order(*to_send[2 * part : 2 * part + 2])
        gather[part] = to_x, to_y, swap(to_x, 2), swap(to_y, 4)

    def gather_forward(part, *also):
        to_x, to_y, from_x, from_y, *also = order(*gather[part], *also)
        shape = (quarter + cut, part_width)
        next_y, next_x = whole(
            gather_forward_kernel, [shape] * 2, to_x, to_y, from_x, from_y, name="gather_forward"
        )
        order.mark(next_y, next_x, *also)
        gather[part] = to_x, from_x, from_y, next_y, next_x, swap(next_y, 4), swap(next_x, 2)
        return also

    def gather_end(part):
        held = order(*gather[part])
        (plane,) = whole(gather_end_kernel, [(4 * short + quarter, part_width)], *held, name="gather_end")
        order.mark(plane)
        return plane

    def grad_step(part, plane, before):
        held = order(plane, out_weight, other_weight, *before)
        share = grad_part(part, *held[:3], held[3:])
        order.mark(*share)
        return share

    piece_width = part_width // 2

    def term_other(piece, plane, attended):
        plane, attended = order(plane, attended)
        shape = (BLOCK, piece_width // SHARES)
        kernel = functools.partial(term_other_kernel, piece % 2 * piece_width)
        share = whole(kernel, [shape] * SHARES, attended, plane, name="term_other")
        order.mark(*share)
        return [swap(transfer, 1) for transfer in share]

    def term_own(piece, plane, attended, arrived):
        held = order(attended, plane, *arrived)
        kernel = functools.partial(term_own_kernel, piece % 2 * piece_width)
        (total,) = whole(kernel, [(BLOCK, piece_width)], *held, name="term_own")
        order.mark(total)
        line.start(piece, total)

    def attend(half):
        held = order(segment_ids, query_rows, key_rows, value_rows)
        attended, there, weights = forward(blocks[4 * half : 4 * half + 4], *held)
        order.mark(attended, there)
        return attended, weights, swap(there, 1)

    def pack(attended, arrived):
        attended, arrived = order(attended, arrived)
        shape = (short + quarter, PAIR)
        packed = whole(pack_kernel, [shape] * 2, attended, arrived, scalars=(blocks,), name="pack")
        order.mark(*packed)
        return packed

    gather_start(0)
    near, weights_near, near_arriving = attend(0)
    far, weights_far, far_arriving = attend(1)
    (other_weight,) = gather_forward(0, other_weight)

    kept, to_x = pack(near, near_arriving)
    from_x = swap(to_x, 2)
    to_y, to_far = pack(far, far_arriving)
    arriving = from_x, swap(to_y, 4), swap(to_far, 6)
    plane = gather_end(0)
    grad = grad_step(0, plane, ())
    held = order(kept, *arriving)
    (gathered,) = whole(collect_kernel, [(4 * short + quarter, PAIR)], *held, name="collect")
    order.mark(gathered)

    arriving = term_other(0, plane, gathered)
    gather_start(1)
    term_own(0, plane, gathered, arriving)
    term_own(1, plane, gathered, term_other(1, plane, gathered))
    gather_forward(1)
    line.across(0)
    plane = gather_end(1)
    term_own(2, plane, gathered, term_other(2, plane, gathered))
    line.across(1)
    arriving = term_other(3, plane, gathered)
    line.back(0)
    term_own(3, plane, gathered, arriving)
    grad_main, grad_extra = grad_step(1, plane, grad)
    held = order(grad_main, grad_extra, swap(grad_extra, 1))
    shape = (rows, PAIR)
    grad_rows = whole(grad_pack_kernel, [shape] * 4, *held, scalars=(blocks,), name="grad_pack")
    order.mark(*grad_rows)
    moved_x, moved_y = swap(grad_rows[1], 2), swap(grad_rows[2], 4)
    line.across(2)
    line.back(1)

    grads = ()

    def finish(i, grad):
        weights = weights_near if i < 2 else weights_far
        held = order(grad, query_rows, key_rows, value_rows, weights)
        result = backward(blocks[2 * i : 2 * i + 2], *held, 2 * (i % 2), grads)
        order.mark(*result)
        return tuple(result)

    grads = finish(0, grad_rows[0])
    line.across(3)
    line.finish(0, 0)
    line.back(2)
    line.finish(1, part_width // 2)
    moved_x, moved_y = order(moved_x, moved_y)
    order.mark(moved_x, moved_y)
    moved_far = swap(order(grad_rows[3]), 6)
    grads = finish(1, moved_x)
    line.back(3)
    grads = finish(2, moved_y)
    line.finish(2, part_width)
    grads = finish(3, moved_far)
    line.finish(3, part_width + part_width // 2)
    return (*grads, *line.done)


def general(query_rows, key_rows, value_rows, out_grad, out_weight, segment_ids):
    rows, width = query_rows.shape
    short = rows // 2
    count = lax.axis_size("fsdp")
    order = jnp.arange(width // BLOCK, dtype=jnp.int32)
    extra = jnp.where((segment_ids[short:] >= 0)[:, None], out_grad[short:], jnp.zeros((), BF16))
    attended, _, weights = forward(order, segment_ids, query_rows, key_rows, value_rows)
    live = jnp.concatenate(
        [lax.all_gather(out_grad[:short], "fsdp", axis=0, tiled=True), lax.psum(extra, "fsdp")]
    )
    attended_live = jnp.concatenate(
        [
            lax.all_to_all(attended[:short], "fsdp", split_axis=1, concat_axis=0, tiled=True),
            lax.psum_scatter(attended[short:], "fsdp", scatter_dimension=1, tiled=True),
        ]
    )
    term = dot(attended_live, live, 0, 0).astype(BF16)
    total = lax.psum(term, "rep").astype(F32)
    grad = dot(live, out_weight, 1, 1).astype(BF16)
    grad_main = lax.all_to_all(
        grad[: count * short], "fsdp", split_axis=0, concat_axis=1, tiled=True
    )
    grad_extra = lax.all_gather(grad[count * short :], "fsdp", axis=1, tiled=True)
    grad = jnp.concatenate([grad_main, grad_extra])
    grads = backward(order, grad, query_rows, key_rows, value_rows, weights, 0, ())
    return (*grads, total * (1.0 / math.sqrt(rows * count * lax.axis_size("rep"))))


def solution(mesh):
    fits = mesh.shape["fsdp"] == 8 and mesh.shape["rep"] == 4
    split = P(("rep", "fsdp"), None)
    return jax.shard_map(
        pairwise if fits else general,
        mesh=mesh,
        in_specs=(split, split, split, split, P("fsdp", None), P(("rep", "fsdp"))),
        out_specs=(split, split, split, P("fsdp", None)),
        check_vma=False,
    )
```

```python
import functools
import math

import jax
import jax.numpy as jnp
from jax import lax
from jax.experimental import pallas as pl
from jax.experimental.pallas import tpu as pltpu
from jax.sharding import PartitionSpec as P

E = 128
BLOCK_HEADS = 3
BLOCK = BLOCK_HEADS * E
PAIR = 2 * BLOCK
PARTS = 2
SHARES = 3
F32 = jnp.float32
BF16 = jnp.bfloat16
LOG2_E = math.log2(math.e)
FAR = -1e30
VMEM_LIMIT = 24 * 1024 * 1024
ATTENTION_VMEM_LIMIT = 40 * 1024 * 1024
NO_COST = pl.CostEstimate(flops=0, bytes_accessed=0, transcendentals=0)


def dot(a, b, a_dim, b_dim):
    return lax.dot_general(a, b, (((a_dim,), (b_dim,)), ((), ())), preferred_element_type=F32)


def forward_kernel(order, ids_column, ids_row, query, key, value, attended, there, weights, bias):
    @pl.when(pl.program_id(0) == 0)
    def _():
        allowed = (ids_column[...] == ids_row[...]) & (ids_column[...] >= 0)
        bias[...] = jnp.where(allowed, 0.0, FAR)

    scale = LOG2_E / math.sqrt(E)
    columns = [slice(head * E, (head + 1) * E) for head in range(BLOCK_HEADS)]
    logits = [dot(key[:, c], query[:, c], 1, 1) * scale + bias[...] for c in columns]
    halves = []
    for head in range(BLOCK_HEADS):
        top = jnp.maximum(jnp.max(logits[head], axis=0, keepdims=True), 0.5 * FAR)
        raw = jnp.exp2(logits[head] - top)
        total = jnp.sum(raw, axis=0, keepdims=True)
        half = (raw * (1.0 / jnp.maximum(total, 0.5))).astype(BF16)
        weights[head] = half
        halves.append(half)
    for head in range(BLOCK_HEADS):
        attended[:, columns[head]] = dot(halves[head], value[:, columns[head]], 0, 0).astype(BF16)
    quarter = there.shape[0]
    start = pl.multiple_of((3 - order[0] % 2) * quarter, 32)
    there[...] = attended[pl.ds(start, quarter), :]


def forward(order, segment_ids, query_rows, key_rows, value_rows):
    rows = query_rows.shape[0]
    blocks = order.shape[0]
    heads = blocks * BLOCK_HEADS
    absolute = pl.BlockSpec((rows, BLOCK), lambda j, order: (0, order[j]))
    return pl.pallas_call(
        forward_kernel,
        grid_spec=pltpu.PrefetchScalarGridSpec(
            num_scalar_prefetch=1,
            grid=(blocks,),
            in_specs=[
                pl.BlockSpec((rows, 1), lambda j, order: (0, 0)),
                pl.BlockSpec((1, rows), lambda j, order: (0, 0)),
                absolute,
                absolute,
                absolute,
            ],
            out_specs=[
                pl.BlockSpec((rows, BLOCK), lambda j, order: (0, j)),
                pl.BlockSpec((rows // 4, BLOCK), lambda j, order: (0, j ^ 1)),
                pl.BlockSpec((BLOCK_HEADS, rows, rows), lambda j, order: (j, 0, 0)),
            ],
            scratch_shapes=[pltpu.VMEM((rows, rows), F32)],
        ),
        out_shape=[
            jax.ShapeDtypeStruct((rows, blocks * BLOCK), BF16),
            jax.ShapeDtypeStruct((rows // 4, blocks * BLOCK), BF16),
            jax.ShapeDtypeStruct((heads, rows, rows), BF16),
        ],
        compiler_params=pltpu.CompilerParams(vmem_limit_bytes=ATTENTION_VMEM_LIMIT),
        cost_estimate=NO_COST,
        name="attention_forward",
    )(order, segment_ids.reshape(rows, 1), segment_ids.reshape(1, rows), query_rows, key_rows, value_rows)


def backward_kernel(order, grad_rows, query, key, value, weights, *rest):
    grad_query, grad_key, grad_value = rest[-3:]
    inverse_root = 1.0 / math.sqrt(E)
    columns = [slice(head * E, (head + 1) * E) for head in range(BLOCK_HEADS)]
    grad_probs = [dot(value[:, c], grad_rows[:, c], 1, 1) for c in columns]
    grad_logits = []
    for head, c in enumerate(columns):
        grad_value[:, c] = dot(weights[head], grad_rows[:, c], 1, 0).astype(BF16)
        wide = weights[head].astype(F32)
        row_dot = jnp.sum(wide * grad_probs[head], axis=0, keepdims=True)
        grad_logits.append((wide * (grad_probs[head] - row_dot)).astype(BF16))
    for head, c in enumerate(columns):
        grad_key[:, c] = (dot(grad_logits[head], query[:, c], 1, 0) * inverse_root).astype(BF16)
    for head, c in enumerate(columns):
        grad_query[:, c] = (dot(grad_logits[head], key[:, c], 0, 0) * inverse_root).astype(BF16)


def backward(order, grad, query_rows, key_rows, value_rows, weights, skip, done):
    rows, width = query_rows.shape
    blocks = order.shape[0]
    heads = blocks * BLOCK_HEADS
    absolute = pl.BlockSpec((rows, BLOCK), lambda j, order: (0, order[j]))
    shapes = [jax.ShapeDtypeStruct((rows, width), BF16)] * 3
    return pl.pallas_call(
        backward_kernel,
        grid_spec=pltpu.PrefetchScalarGridSpec(
            num_scalar_prefetch=1,
            grid=(blocks,),
            in_specs=[
                pl.BlockSpec((rows, BLOCK), lambda j, order: (0, j)),
                absolute,
                absolute,
                absolute,
                pl.BlockSpec((BLOCK_HEADS, rows, rows), lambda j, order: (j + skip, 0, 0)),
            ]
            + [pl.BlockSpec(memory_space=pl.ANY)] * len(done),
            out_specs=[absolute, absolute, absolute],
        ),
        out_shape=shapes,
        input_output_aliases={6 + i: i for i in range(len(done))},
        compiler_params=pltpu.CompilerParams(vmem_limit_bytes=ATTENTION_VMEM_LIMIT),
        cost_estimate=NO_COST,
        name="attention_backward",
    )(order, grad, query_rows, key_rows, value_rows, weights, *done)


def whole(kernel, shapes, *arrays, scalars=(), name):
    vmem, smem = pl.BlockSpec(memory_space=pltpu.VMEM), pl.BlockSpec(memory_space=pltpu.SMEM)
    return pl.pallas_call(
        kernel,
        in_specs=[smem] * len(scalars) + [vmem] * len(arrays),
        out_specs=[vmem] * len(shapes),
        out_shape=[jax.ShapeDtypeStruct(shape, BF16) for shape in shapes],
        compiler_params=pltpu.CompilerParams(vmem_limit_bytes=VMEM_LIMIT),
        cost_estimate=NO_COST,
        name=name,
    )(*scalars, *arrays)


def other_quarter_kernel(blocks, ids, extra, out):
    is_full = ids[ids.shape[0] - 1] >= 0
    out[...] = jnp.where(is_full, extra[...], jnp.zeros((), BF16))


def other_quarter(blocks, ids, rows):
    count, width = rows.shape
    quarter = count // 4
    return pl.pallas_call(
        other_quarter_kernel,
        grid_spec=pltpu.PrefetchScalarGridSpec(
            num_scalar_prefetch=2,
            grid=(1,),
            in_specs=[pl.BlockSpec((quarter, width), lambda i, blocks, ids: (3 - blocks[0] % 2, 0))],
            out_specs=pl.BlockSpec((quarter, width), lambda i, blocks, ids: (0, 0)),
        ),
        out_shape=jax.ShapeDtypeStruct((quarter, width), BF16),
        compiler_params=pltpu.CompilerParams(vmem_limit_bytes=ATTENTION_VMEM_LIMIT),
        cost_estimate=NO_COST,
        name="other_quarter",
    )(blocks, ids, rows)


def gather_start_kernel(blocks, ids, rows, arrived, *outs):
    quarter = arrived.shape[0]
    short, cut = 2 * quarter, quarter // 2
    is_full = ids[ids.shape[0] - 1] >= 0
    start = pl.multiple_of(short + quarter * (blocks[0] % 2), 32)
    own = jnp.where(is_full, rows[pl.ds(start, quarter), :], jnp.zeros((), BF16))
    here = own + arrived[...]
    width = outs[0].shape[1]
    for part in range(len(outs) // 2):
        columns = slice(part * width, (part + 1) * width)
        for i in range(2):
            outs[2 * part + i][:short] = rows[:short, columns]
            outs[2 * part + i][short:] = here[i * cut : (i + 1) * cut, columns]


def gather_forward_kernel(to_x, to_y, from_x, from_y, next_y, next_x):
    quarter = from_x.shape[0] * 2 // 5
    short = 2 * quarter
    next_y[:quarter] = from_x[:quarter]
    next_x[:quarter] = from_y[quarter:short]
    next_y[quarter:] = to_x[short:] + from_x[short:]
    next_x[quarter:] = to_y[short:] + from_y[short:]


def gather_end_kernel(to_x, from_x, from_y, next_y, next_x, via_y, via_x, plane):
    quarter = to_x.shape[0] * 2 // 5
    short, cut = 2 * quarter, quarter // 2
    plane[:short] = to_x[:short]
    plane[short : 2 * short] = from_x[:short]
    plane[2 * short : 3 * short] = from_y[:short]
    plane[3 * short : 3 * short + quarter] = via_y[:quarter]
    plane[3 * short + quarter : 4 * short] = via_x[:quarter]
    plane[4 * short : 4 * short + cut] = next_y[quarter:] + via_y[quarter:]
    plane[4 * short + cut :] = next_x[quarter:] + via_x[quarter:]


def pack_kernel(blocks, attended, arrived, *outs):
    quarter = arrived.shape[0]
    short = 2 * quarter
    start = pl.multiple_of(short + quarter * (blocks[0] % 2), 32)
    extra = attended[pl.ds(start, quarter), :] + arrived[...]
    for i, out in enumerate(outs):
        columns = slice(i * PAIR, (i + 1) * PAIR)
        out[:short] = attended[:short, columns]
        out[short:] = extra[:, columns]


def collect_kernel(kept, from_x, from_y, from_far, gathered):
    short = kept.shape[0] * 2 // 3
    parts = [kept, from_x, from_y, from_far]
    for i, part in enumerate(parts):
        gathered[i * short : (i + 1) * short] = part[:short]
    gathered[4 * short :] = (kept[short:] + from_x[short:]) + (from_y[short:] + from_far[short:])


def term_other_kernel(begin, attended, plane, *outs):
    width = outs[0].shape[1]
    share = dot(attended[:, BLOCK:], plane[:, begin : begin + len(outs) * width], 0, 0).astype(BF16)
    for i, out in enumerate(outs):
        out[...] = share[:, i * width : (i + 1) * width]


def term_own_kernel(begin, attended, plane, *refs):
    arrived, out = refs[:-1], refs[-1]
    own = dot(attended[:, :BLOCK], plane[:, begin : begin + out.shape[1]], 0, 0)
    there = jnp.concatenate([a[...] for a in arrived], axis=1)
    out[...] = (own + there.astype(F32)).astype(BF16)


def grad_kernel(plane, own, other, *rest):
    for i, weight in enumerate((own, other)):
        columns = slice(i * BLOCK, (i + 1) * BLOCK)
        share = dot(plane[...], weight[...], 1, 1)
        if len(rest) == 2:
            share = rest[0][:, columns] + share
        rest[-1][:, columns] = share


def grad_end_kernel(plane, own, other, before, main, extra):
    rows = main.shape[0]
    for i, weight in enumerate((own, other)):
        columns = slice(i * BLOCK, (i + 1) * BLOCK)
        total = (before[:, columns] + dot(plane[...], weight[...], 1, 1)).astype(BF16)
        main[:, columns] = total[:rows]
        extra[:, columns] = total[rows:]


def grad_pack_kernel(blocks, main, extra, arrived, *outs):
    short = main.shape[0] // len(outs)
    quarter = extra.shape[0]
    first = blocks[0] % 2 == 0
    there = jnp.concatenate([arrived[:, BLOCK:], arrived[:, :BLOCK]], axis=1)
    for i, out in enumerate(outs):
        out[:short] = main[i * short : (i + 1) * short]
        out[short : short + quarter] = jnp.where(first, extra[...], there)
        out[short + quarter :] = jnp.where(first, there, extra[...])


def grad_part(part, plane, own_weight, other_weight, before):
    count, width = plane.shape
    weight = pl.BlockSpec((BLOCK, width), lambda i: (0, part))
    result = pl.BlockSpec((count, PAIR), lambda i: (0, 0))
    last = part == PARTS - 1
    extra = count // 9
    outs = [(count - extra, PAIR), (extra, PAIR)]
    return pl.pallas_call(
        grad_end_kernel if last else grad_kernel,
        grid=(1,),
        in_specs=[pl.BlockSpec((count, width), lambda i: (0, 0)), weight, weight] + [result] * len(before),
        out_specs=[pl.BlockSpec(shape, lambda i: (0, 0)) for shape in outs] if last else [result],
        out_shape=[jax.ShapeDtypeStruct(shape, BF16) for shape in outs]
        if last
        else [jax.ShapeDtypeStruct((count, PAIR), F32)],
        compiler_params=pltpu.CompilerParams(vmem_limit_bytes=VMEM_LIMIT),
        cost_estimate=NO_COST,
        name="grad_attended",
    )(plane, own_weight, other_weight, *before)


def add_kernel(a, b, out):
    out[...] = (a[...].astype(F32) + b[...].astype(F32)).astype(BF16)


class Order:
    def __init__(self):
        self.last = ()

    def __call__(self, *arrays):
        held = lax.optimization_barrier((*self.last, *arrays))[len(self.last) :]
        return held[0] if len(held) == 1 else held

    def mark(self, *arrays):
        self.last = tuple(arrays)


def add(a, b):
    return whole(add_kernel, [a.shape], a, b, name="add")[0]


def line_end_kernel(scale, place, total, arrived, *rest):
    in_middle = (place[0] == 1) | (place[0] == 2)
    rest[-1][...] = jnp.where(in_middle, total[...], arrived[...]).astype(F32) * scale


def line_end(scale, place, total, arrived, start, all_width, done):
    rows, width = total.shape
    piece = pl.BlockSpec((rows, width), lambda i, place: (0, 0))
    return pl.pallas_call(
        functools.partial(line_end_kernel, scale),
        grid_spec=pltpu.PrefetchScalarGridSpec(
            num_scalar_prefetch=1,
            grid=(1,),
            in_specs=[piece, piece] + [pl.BlockSpec(memory_space=pl.ANY)] * len(done),
            out_specs=pl.BlockSpec((rows, width), lambda i, place: (0, start // width)),
        ),
        out_shape=jax.ShapeDtypeStruct((rows, all_width), F32),
        input_output_aliases={3 + i: i for i in range(len(done))},
        compiler_params=pltpu.CompilerParams(vmem_limit_bytes=VMEM_LIMIT),
        cost_estimate=NO_COST,
        name="line_end",
    )(place, total, arrived, *done)


class LineSum:
    def __init__(self, order, scale, width):
        self.order, self.scale, self.width = order, scale, width
        self.place = lax.axis_index("rep").astype(jnp.int32).reshape(1)
        self.held, self.arriving, self.done = {}, {}, ()

    def start(self, piece, part):
        self.held[piece] = part
        self.arriving[piece] = lax.ppermute(part, "rep", [(0, 1), (3, 2)])

    def across(self, piece):
        part, arrived = self.order(self.held[piece], self.arriving[piece])
        pair = add(part, arrived)
        self.order.mark(pair)
        self.held[piece] = pair
        self.arriving[piece] = lax.ppermute(pair, "rep", [(1, 2), (2, 1)])

    def back(self, piece):
        pair, arrived = self.order(self.held[piece], self.arriving[piece])
        total = add(pair, arrived)
        self.order.mark(total)
        self.held[piece] = total
        self.arriving[piece] = lax.ppermute(total, "rep", [(1, 0), (2, 3)])

    def finish(self, piece, start):
        held = self.order(self.held[piece], self.arriving[piece], *self.done)
        result = line_end(self.scale, self.place, held[0], held[1], start, self.width, held[2:])
        self.order.mark(result)
        self.done = (result,)


def pairwise(query_rows, key_rows, value_rows, out_grad, out_weight, segment_ids):
    rows, width = query_rows.shape
    short = rows // 2
    quarter = short // 2
    cut = quarter // 2
    part_width = width // PARTS
    me = lax.axis_index("fsdp")
    core = me % 2
    blocks = me ^ jnp.arange(8, dtype=jnp.int32)
    order = Order()
    line = LineSum(order, 1.0 / math.sqrt(rows * lax.axis_size("fsdp") * lax.axis_size("rep")), width)

    def swap(a, mask):
        return lax.ppermute(a, "fsdp", [(f, f ^ mask) for f in range(8)])

    other_weight = swap(out_weight, 1)

    there = other_quarter(blocks, segment_ids, out_grad)
    order.mark(there)
    arrived_extra = swap(there, 1)

    ids, rows_held, arrived = order(segment_ids, out_grad, arrived_extra)
    shape = (short + cut, part_width)
    to_send = whole(
        gather_start_kernel, [shape] * (2 * PARTS), rows_held, arrived, scalars=(blocks, ids), name="gather_start"
    )
    order.mark(*to_send)
    gather = {}

    def gather_start(part):
        to_x, to_y = order(*to_send[2 * part : 2 * part + 2])
        gather[part] = to_x, to_y, swap(to_x, 2), swap(to_y, 4)

    def gather_forward(part, *also):
        to_x, to_y, from_x, from_y, *also = order(*gather[part], *also)
        shape = (quarter + cut, part_width)
        next_y, next_x = whole(
            gather_forward_kernel, [shape] * 2, to_x, to_y, from_x, from_y, name="gather_forward"
        )
        order.mark(next_y, next_x, *also)
        gather[part] = to_x, from_x, from_y, next_y, next_x, swap(next_y, 4), swap(next_x, 2)
        return also

    def gather_end(part):
        held = order(*gather[part])
        (plane,) = whole(gather_end_kernel, [(4 * short + quarter, part_width)], *held, name="gather_end")
        order.mark(plane)
        return plane

    def grad_step(part, plane, before):
        held = order(plane, out_weight, other_weight, *before)
        share = grad_part(part, *held[:3], held[3:])
        order.mark(*share)
        return share

    piece_width = part_width // 2

    def term_other(piece, plane, attended):
        plane, attended = order(plane, attended)
        shape = (BLOCK, piece_width // SHARES)
        kernel = functools.partial(term_other_kernel, piece % 2 * piece_width)
        share = whole(kernel, [shape] * SHARES, attended, plane, name="term_other")
        order.mark(*share)
        return [swap(transfer, 1) for transfer in share]

    def term_own(piece, plane, attended, arrived):
        held = order(attended, plane, *arrived)
        kernel = functools.partial(term_own_kernel, piece % 2 * piece_width)
        (total,) = whole(kernel, [(BLOCK, piece_width)], *held, name="term_own")
        order.mark(total)
        line.start(piece, total)

    def attend(half):
        held = order(segment_ids, query_rows, key_rows, value_rows)
        attended, there, weights = forward(blocks[4 * half : 4 * half + 4], *held)
        order.mark(attended, there)
        return attended, weights, swap(there, 1)

    def pack(attended, arrived):
        attended, arrived = order(attended, arrived)
        shape = (short + quarter, PAIR)
        packed = whole(pack_kernel, [shape] * 2, attended, arrived, scalars=(blocks,), name="pack")
        order.mark(*packed)
        return packed

    gather_start(0)
    near, weights_near, near_arriving = attend(0)
    far, weights_far, far_arriving = attend(1)
    (other_weight,) = gather_forward(0, other_weight)

    kept, to_x = pack(near, near_arriving)
    from_x = swap(to_x, 2)
    to_y, to_far = pack(far, far_arriving)
    arriving = from_x, swap(to_y, 4), swap(to_far, 6)
    plane = gather_end(0)
    grad = grad_step(0, plane, ())
    held = order(kept, *arriving)
    (gathered,) = whole(collect_kernel, [(4 * short + quarter, PAIR)], *held, name="collect")
    order.mark(gathered)

    arriving = term_other(0, plane, gathered)
    gather_start(1)
    term_own(0, plane, gathered, arriving)
    term_own(1, plane, gathered, term_other(1, plane, gathered))
    gather_forward(1)
    line.across(0)
    plane = gather_end(1)
    term_own(2, plane, gathered, term_other(2, plane, gathered))
    line.across(1)
    arriving = term_other(3, plane, gathered)
    line.back(0)
    term_own(3, plane, gathered, arriving)
    line.across(2)
    grad_main, grad_extra = grad_step(1, plane, grad)
    held = order(grad_main, grad_extra, swap(grad_extra, 1))
    shape = (rows, PAIR)
    grad_rows = whole(grad_pack_kernel, [shape] * 4, *held, scalars=(blocks,), name="grad_pack")
    order.mark(*grad_rows)
    moved_x, moved_y = swap(grad_rows[1], 2), swap(grad_rows[2], 4)
    line.back(1)

    grads = ()

    def finish(i, grad):
        weights = weights_near if i < 2 else weights_far
        held = order(grad, query_rows, key_rows, value_rows, weights)
        result = backward(blocks[2 * i : 2 * i + 2], *held, 2 * (i % 2), grads)
        order.mark(*result)
        return tuple(result)

    grads = finish(0, grad_rows[0])
    line.across(3)
    line.finish(0, 0)
    line.back(2)
    line.finish(1, part_width // 2)
    moved_x, moved_y = order(moved_x, moved_y)
    order.mark(moved_x, moved_y)
    moved_far = swap(order(grad_rows[3]), 6)
    grads = finish(1, moved_x)
    line.back(3)
    grads = finish(2, moved_y)
    line.finish(2, part_width)
    grads = finish(3, moved_far)
    line.finish(3, part_width + part_width // 2)
    return (*grads, *line.done)


def general(query_rows, key_rows, value_rows, out_grad, out_weight, segment_ids):
    rows, width = query_rows.shape
    short = rows // 2
    count = lax.axis_size("fsdp")
    order = jnp.arange(width // BLOCK, dtype=jnp.int32)
    extra = jnp.where((segment_ids[short:] >= 0)[:, None], out_grad[short:], jnp.zeros((), BF16))
    attended, _, weights = forward(order, segment_ids, query_rows, key_rows, value_rows)
    live = jnp.concatenate(
        [lax.all_gather(out_grad[:short], "fsdp", axis=0, tiled=True), lax.psum(extra, "fsdp")]
    )
    attended_live = jnp.concatenate(
        [
            lax.all_to_all(attended[:short], "fsdp", split_axis=1, concat_axis=0, tiled=True),
            lax.psum_scatter(attended[short:], "fsdp", scatter_dimension=1, tiled=True),
        ]
    )
    term = dot(attended_live, live, 0, 0).astype(BF16)
    total = lax.psum(term, "rep").astype(F32)
    grad = dot(live, out_weight, 1, 1).astype(BF16)
    grad_main = lax.all_to_all(
        grad[: count * short], "fsdp", split_axis=0, concat_axis=1, tiled=True
    )
    grad_extra = lax.all_gather(grad[count * short :], "fsdp", axis=1, tiled=True)
    grad = jnp.concatenate([grad_main, grad_extra])
    grads = backward(order, grad, query_rows, key_rows, value_rows, weights, 0, ())
    return (*grads, total * (1.0 / math.sqrt(rows * count * lax.axis_size("rep"))))


def solution(mesh):
    fits = mesh.shape["fsdp"] == 8 and mesh.shape["rep"] == 4
    split = P(("rep", "fsdp"), None)
    return jax.shard_map(
        pairwise if fits else general,
        mesh=mesh,
        in_specs=(split, split, split, split, P("fsdp", None), P(("rep", "fsdp"))),
        out_specs=(split, split, split, P("fsdp", None)),
        check_vma=False,
    )
```
